128 devices in a mesh: region: 16 (over z, y), sub: 8 (over x, core).
Axes of the slice: x: 4, y: 4, z: 4, core: 2. Of those that a mesh axis runs over, the one named last changes fastest.
Arguments:
- tokens: bfloat16 [131072, 1024], P(('region', 'sub')), may hold values from -6 to 6
- nodes: bfloat16 [20480, 1024], P(('region', 'sub')), may hold values from -6 to 6
- dests: int32 [131072, 2], P(('region', 'sub')), may hold values from 0 to 20479, as said below
- token_count: int32 [128], P(('region', 'sub')), may hold values from 256 to 1024, as said below
- w_src: bfloat16 [1024, 1024], replicated, may hold values from -0.1875 to 0.1875
- w_dst: bfloat16 [1024, 1024], replicated, may hold values from -0.1875 to 0.1875
- bias: float32 [1024], replicated, may hold values from -4 to 4
- w_out: bfloat16 [1024, 1024], replicated, may hold values from -0.1875 to 0.1875
- cotangent: bfloat16 [20480, 1024], P(('region', 'sub')), may hold values from -6 to 6
Outputs:
- updated: bfloat16 [20480, 1024], P(('region', 'sub'))
- token_grad: bfloat16 [131072, 1024], P(('region', 'sub'))
- node_grad: bfloat16 [20480, 1024], P(('region', 'sub'))
- grad_src: float32 [1024, 1024], P(('region', 'sub'))
- grad_dst: float32 [1024, 1024], P(('region', 'sub'))
- grad_out: float32 [1024, 1024], P(('region', 'sub'))
- grad_bias: float32 [1024], P(('region', 'sub'))
The draws below stay inside these ranges and needn't reach their ends.
Inputs may be any that keep to these rules, and one draw needn't show every extreme that they name: `dests`: node block of device d (d = region index * 8 + sub index) is rows d * 160 to (d + 1) * 160 - 1. Every edge of a token of device (r, s) points into the node block of (r, s), (r - 1, s), (r + 1, s), (r, s - 1) or (r, s + 1), among those that exist. `token_count`: some device has all 1024 slots live.
All inputs are finite; a program needn't handle non-finite values.
Results may differ from the reference program's by a relative error of at most 0.012.
Values may be sent and summed in bfloat16 or wider, within the bound.
A program may use at most 128 MiB of HBM per device.

```python
import jax
import jax.numpy as jnp
from jax import lax

D = 1024
H = 1024
K = 2
TOK_DEV = 1024
NODE_DEV = 160
TOKENS = 131072
NODES = 20480
N_REGION = 16
N_SUB = 8
DEVICES = 128


def draw_dests(key, part):
    key = jax.random.fold_in(key, 11)
    key_pick, key_local = jax.random.split(key)
    owner = jnp.arange(TOKENS, dtype=jnp.int32) // TOK_DEV
    row_pos = (owner // N_SUB)[:, None]
    col_pos = (owner % N_SUB)[:, None]
    pick = jax.random.randint(key_pick, (TOKENS, K), 0, 8)
    step_row = jnp.where(pick == 4, -1, jnp.where(pick == 5, 1, 0))
    step_col = jnp.where(pick == 6, -1, jnp.where(pick == 7, 1, 0))
    new_row = row_pos + step_row
    new_col = col_pos + step_col
    inside = (new_row >= 0) & (new_row < N_REGION) & (new_col >= 0) & (new_col < N_SUB)
    new_row = jnp.where(inside, new_row, row_pos)
    new_col = jnp.where(inside, new_col, col_pos)
    local = jax.random.randint(key_local, (TOKENS, K), 0, NODE_DEV)
    return ((new_row * N_SUB + new_col) * NODE_DEV + local).astype(jnp.int32)


def draw_token_count(key, part):
    key = jax.random.fold_in(key, 5)
    key_raw, key_heavy = jax.random.split(key)
    lowest = TOK_DEV // 4
    spread = TOK_DEV - lowest
    raw = jax.random.randint(key_raw, (DEVICES,), 0, spread + 1)
    counts = lowest + raw * raw // max(spread, 1)
    heavy = jax.random.randint(key_heavy, (), 0, DEVICES)
    return jnp.where(jnp.arange(DEVICES) == heavy, TOK_DEV, counts).astype(jnp.int32)


def level_of(key, shape, cuts, smallest, top_value):
    loudness, own = 1.0, jax.random.fold_in(key, 6)
    for dim, parts in cuts:
        draws = jnp.exp(jax.random.uniform(jax.random.fold_in(own, dim), (parts,), jnp.float32, smallest / len(cuts), top_value / len(cuts)))
        loudness = loudness * jnp.repeat(draws, shape[dim] // parts).reshape([-1 if axis == dim else 1 for axis in range(len(shape))])
    return loudness


def normal_values(rng, shape, deviation, reach, shards=(), held_as=jnp.bfloat16):
    array = deviation * jax.random.normal(rng, shape, jnp.float32)
    if shards:
        array = array * level_of(rng, shape, shards, -0.22, 0.18)
    return jnp.clip(array, -reach, reach).astype(held_as)


def setup_inputs(seed: int = 0) -> dict:
    key_list = jax.random.split(jax.random.key(seed), 10)
    tokens = normal_values(key_list[0], (TOKENS, D), 1.0, 6.0, ((0, 128),))
    nodes = normal_values(key_list[1], (NODES, D), 1.0, 6.0, ((0, 128),))
    dests = draw_dests(jax.random.fold_in(key_list[9], 71), 0)
    token_count = draw_token_count(jax.random.fold_in(key_list[9], 71), 0)
    w_src = normal_values(key_list[4], (D, H), D ** -0.5, 0.1875)
    w_dst = normal_values(key_list[5], (D, H), D ** -0.5, 0.1875)
    bias = normal_values(key_list[6], (H,), 1.0, 4.0, (), jnp.float32)
    w_out = normal_values(key_list[7], (H, D), H ** -0.5, 0.1875)
    cotangent = normal_values(key_list[8], (NODES, D), 1.0, 6.0, ((0, 128),))
    return {"tokens": tokens, "nodes": nodes, "dests": dests, "token_count": token_count, "w_src": w_src, "w_dst": w_dst, "bias": bias, "w_out": w_out, "cotangent": cotangent}


def reference(tokens, nodes, dests, token_count, w_src, w_dst, bias, w_out, cotangent):
    f32 = jnp.float32
    bf16 = jnp.bfloat16
    node_proj = jnp.dot(nodes, w_dst, preferred_element_type=f32).astype(bf16)
    node_up = jnp.dot(cotangent, w_out.T, preferred_element_type=f32).astype(bf16)
    width = (2 * N_SUB + 1) * NODE_DEV

    def add_window(buffer, first, partial_value):
        window = lax.dynamic_slice_in_dim(buffer, first, width, 0)
        return lax.dynamic_update_slice_in_dim(buffer, window + partial_value, first, 0)

    def device_step(state, device):
        seg_fwd, seg_bwd, grad_src, grad_bias = state
        x_rows = lax.dynamic_slice_in_dim(tokens, device * TOK_DEV, TOK_DEV, 0)
        targets = lax.dynamic_slice_in_dim(dests, device * TOK_DEV, TOK_DEV, 0)
        live = (jnp.arange(TOK_DEV, dtype=jnp.int32) < token_count[device]).astype(f32)[:, None, None]
        token_proj = jnp.dot(x_rows, w_src, preferred_element_type=f32)
        preact = token_proj[:, None, :] + node_proj[targets].astype(f32) + bias
        sigma = jax.nn.sigmoid(preact)
        edge_act = (jax.nn.silu(preact) * live).astype(bf16)
        edge_grad = (node_up[targets].astype(f32) * sigma * (1.0 + preact * (1.0 - sigma)) * live).astype(bf16)
        first = (jnp.clip(device - N_SUB, 0, DEVICES - 2 * N_SUB - 1) * NODE_DEV).astype(jnp.int32)
        local = (targets - first).reshape(-1).astype(jnp.int32)
        part_fwd = jax.ops.segment_sum(edge_act.reshape(-1, H).astype(f32), local, num_segments=width)
        part_fwd = lax.optimization_barrier(part_fwd.astype(bf16)).astype(f32)
        part_bwd = jax.ops.segment_sum(edge_grad.reshape(-1, H).astype(f32), local, num_segments=width)
        part_bwd = lax.optimization_barrier(part_bwd.astype(bf16)).astype(f32)
        seg_fwd = add_window(seg_fwd, first, part_fwd)
        seg_bwd = add_window(seg_bwd, first, part_bwd)
        token_back = jnp.sum(edge_grad.astype(f32), axis=1).astype(bf16)
        x_grad = jnp.dot(token_back, w_src.T, preferred_element_type=f32).astype(bf16)
        grad_src = grad_src + jnp.dot(x_rows.T, token_back, preferred_element_type=f32)
        grad_bias = grad_bias + jnp.sum(edge_grad.astype(f32), axis=(0, 1))
        return (seg_fwd, seg_bwd, grad_src, grad_bias), x_grad

    start_state = (jnp.zeros((NODES, H), f32), jnp.zeros((NODES, H), f32),
                   jnp.zeros((D, H), f32), jnp.zeros((H,), f32))
    final_state, grads_rows = lax.scan(device_step, start_state, jnp.arange(DEVICES, dtype=jnp.int32))
    seg_fwd, seg_bwd, grad_src, grad_bias = final_state
    node_sum = seg_fwd.astype(bf16)
    node_back = seg_bwd.astype(bf16)
    updated = (nodes.astype(f32) + jnp.dot(node_sum, w_out, preferred_element_type=f32)).astype(bf16)
    token_grad = grads_rows.reshape(TOKENS, D)
    node_grad = (cotangent.astype(f32) + jnp.dot(node_back, w_dst.T, preferred_element_type=f32)).astype(bf16)
    grad_dst = jnp.dot(nodes.T, node_back, preferred_element_type=f32)
    grad_out = jnp.dot(node_sum.T, cotangent, preferred_element_type=f32)
    return updated, token_grad, node_grad, grad_src, grad_dst, grad_out, grad_bias
```

```python
import jax
import jax.numpy as jnp
from jax import lax
from jax.experimental import pallas as pl
from jax.experimental.pallas import tpu as pltpu
from jax.sharding import PartitionSpec as P

MESH = pl.DeviceIdType.MESH
ROUND = (0, 1, 2)
ORDERS = ((0, 2, 1), (2, 1, 0), (1, 0, 2))
BIAS_ORDER = (2, 1, 0)


def device_at(coords, core):
    return (coords[0] * 4 + coords[1], coords[2] * 2 + core)


def moved(coords, dim, value):
    return tuple(value if d == dim else c for d, c in enumerate(coords))


def pick(blocks):
    return tuple(blocks.get(d, slice(None)) for d in ROUND)


def partner(half, position):
    return position + 1 - 2 * (position % 2) if half == 0 else 3 - position


def mesh_position():
    region, sub = lax.axis_index("region"), lax.axis_index("sub")
    return (region // 4, region % 4, sub // 2), sub % 2


def reduce_kernel(
    src_ref, dst_ref, out_ref, bias_ref, o_src, o_dst, o_out, o_bias,
    acc, pair, r1, r2, r3, r4, fin, fin_r, b_acc, b_r,
    load_sem, pair_s, pair_v, s1, v1, s2, v2, s3, v3, s4, v4, fin_s, fin_v, b_s, b_v,
):
    f32, bf16 = jnp.float32, jnp.bfloat16
    mats, outs = (src_ref, dst_ref, out_ref), (o_src, o_dst, o_out)
    coords, core = mesh_position()
    mine = pl.ds(pl.multiple_of(core * 512, 512), 512)
    theirs = pl.ds(pl.multiple_of((1 - core) * 512, 512), 512)
    twin = device_at(coords, 1 - core)
    ring = [
        [device_at(moved(coords, dim, (coords[dim] + hop) % 4), core) for hop in (1, 2, 3)]
        for dim in ROUND
    ]
    cols = (pl.ds(0, 256), pl.ds(256, 256))
    sends = []

    def remote(source, target, send, recv, device):
        return pltpu.make_async_remote_copy(
            src_ref=source, dst_ref=target, send_sem=send, recv_sem=recv,
            device_id=device, device_id_type=MESH,
        )

    def go(copy):
        copy.start()
        sends.append(copy)
        return copy

    for m in range(3):
        pltpu.make_async_copy(mats[m].at[:, :, :, :, mine], acc.at[m], load_sem.at[m]).start()
    barrier = pltpu.get_barrier_semaphore()
    peers = [twin] + ring[0] + ring[1] + ring[2]
    for peer in peers:
        pl.semaphore_signal(barrier, inc=1, device_id=peer, device_id_type=MESH)
    pl.semaphore_wait(barrier, len(peers))

    pairs = [
        go(remote(mats[m].at[:, :, :, :, theirs], pair.at[m], pair_s.at[m], pair_v.at[m], twin))
        for m in range(3)
    ]

    def step_one(m):
        dim = ORDERS[m][0]
        p = coords[dim]
        copies = []
        for half in range(2):
            q = partner(half, p)
            device = device_at(moved(coords, dim, q), core)
            for slot, block in ((1, partner(1 - half, q)), (0, q)):
                copies.append(go(remote(
                    acc.at[(m, *pick({dim: block}), slice(None), cols[half])],
                    r1.at[m, half, slot], s1.at[m, half, slot], v1.at[m, half, slot], device,
                )))
        return copies

    def add_in(m, blocks, half, value_ref):
        where = (m, *pick(blocks), slice(None), cols[half])
        acc[where] = (acc[where].astype(f32) + value_ref[...].astype(f32)).astype(bf16)

    def step_two(m, copies):
        dim = ORDERS[m][0]
        p = coords[dim]
        started = []
        for half in range(2):
            copies[2 * half].wait_recv()
            q = partner(1 - half, p)
            add_in(m, {dim: q}, half, r1.at[m, half, 1])
            started.append(go(remote(
                acc.at[(m, *pick({dim: q}), slice(None), cols[half])],
                r2.at[m, half], s2.at[m, half], v2.at[m, half],
                device_at(moved(coords, dim, q), core),
            )))
        for half in range(2):
            copies[2 * half + 1].wait_recv()
            add_in(m, {dim: p}, half, r1.at[m, half, 0])
        return started

    def step_three(m, copies):
        first, dim = ORDERS[m][0], ORDERS[m][1]
        p = coords[first]
        for half in range(2):
            copies[half].wait_recv()
            add_in(m, {first: p}, half, r2.at[m, half])
        started = []
        for hop in (2, 1, 3):
            block = (coords[dim] + hop) % 4
            started.append(go(remote(
                acc.at[(m, *pick({first: p, dim: block}))],
                r3.at[m, hop - 1], s3.at[m, hop - 1], v3.at[m, hop - 1], ring[dim][hop - 1],
            )))
        return started

    def step_four(m, copies):
        first, second, dim = ORDERS[m]
        for copy in copies:
            copy.wait_recv()
        where = (m, *pick({first: coords[first], second: coords[second]}))
        total = acc[where].astype(f32)
        for slot in range(3):
            total = total + r3[m, slot].astype(f32)
        acc[where] = total.astype(bf16)
        started = []
        for hop in (2, 1, 3):
            block = (coords[dim] + hop) % 4
            started.append(go(remote(
                acc.at[(m, *pick({first: coords[first], second: coords[second], dim: block}))],
                r4.at[m, hop - 1], s4.at[m, hop - 1], v4.at[m, hop - 1], ring[dim][hop - 1],
            )))
        return started

    def step_five(m, copies):
        for copy in copies:
            copy.wait_recv()
        total = acc[(m, *coords)].astype(f32)
        for slot in range(3):
            total = total + r4[m, slot].astype(f32)
        fin[m, 0] = total[:8]
        fin[m, 1] = total[8:]
        return go(remote(fin.at[m, 1 - core], fin_r.at[m], fin_s.at[m], fin_v.at[m], twin))

    def bias_send(stage):
        if stage == 3:
            return [go(remote(b_acc.at[3], b_r.at[9], b_s.at[9], b_v.at[9], twin))]
        started = []
        for hop in range(3):
            slot = 3 * stage + hop
            started.append(go(remote(
                b_acc.at[stage], b_r.at[slot], b_s.at[slot], b_v.at[slot],
                ring[BIAS_ORDER[stage]][hop],
            )))
        return started

    def bias_add(stage, copies):
        total = b_acc[stage]
        for copy in copies:
            copy.wait_recv()
        for slot in range(3 * stage, 3 * stage + len(copies)):
            total = total + b_r[slot]
        return total

    b_acc[0] = bias_ref[...]
    b_copies = bias_send(0)
    state = []
    for m in range(3):
        pltpu.make_async_copy(mats[m].at[:, :, :, :, mine], acc.at[m], load_sem.at[m]).wait()
        pairs[m].wait_recv()

        def add_rows(i, carry, m=m):
            z, y = i // 4, i % 4
            acc[m, z, y] = (acc[m, z, y].astype(f32) + pair[m, z, y].astype(f32)).astype(bf16)
            return carry

        lax.fori_loop(0, 16, add_rows, 0)
        state.append(step_one(m))
    b_acc[1] = bias_add(0, b_copies)
    b_copies = bias_send(1)
    state = [step_two(m, state[m]) for m in range(3)]
    b_acc[2] = bias_add(1, b_copies)
    b_copies = bias_send(2)
    state = [step_three(m, state[m]) for m in range(3)]
    b_acc[3] = bias_add(2, b_copies)
    b_copies = bias_send(3)
    state = [step_four(m, state[m]) for m in range(3)]
    state = [step_five(m, state[m]) for m in range(3)]
    o_bias[...] = bias_add(3, b_copies)
    for m in range(3):
        state[m].wait_recv()
        outs[m][:, mine] = fin[m, core]
        outs[m][:, theirs] = fin_r[m]
    for copy in sends:
        copy.wait_send()


def reduce_scatter(src, dst, out, bias):
    f32, bf16 = jnp.float32, jnp.bfloat16
    dma = pltpu.SemaphoreType.DMA
    vmem = pl.BlockSpec(memory_space=pltpu.VMEM)
    hbm = pl.BlockSpec(memory_space=pl.ANY)
    view = (4, 4, 4, 16, 1024)
    slab = jax.ShapeDtypeStruct((8, 1024), f32)
    o_src, o_dst, o_out, o_bias = pl.pallas_call(
        reduce_kernel,
        out_shape=(slab, slab, slab, jax.ShapeDtypeStruct((8, 128), f32)),
        in_specs=[hbm, hbm, hbm, vmem],
        out_specs=[vmem] * 4,
        scratch_shapes=[
            pltpu.VMEM((3, 4, 4, 4, 16, 512), bf16),
            pltpu.VMEM((3, 4, 4, 4, 16, 512), bf16),
            pltpu.VMEM((3, 2, 2, 4, 4, 16, 256), bf16),
            pltpu.VMEM((3, 2, 4, 4, 16, 256), bf16),
            pltpu.VMEM((3, 3, 4, 16, 512), bf16),
            pltpu.VMEM((3, 3, 16, 512), bf16),
            pltpu.VMEM((3, 2, 8, 512), f32),
            pltpu.VMEM((3, 8, 512), f32),
            pltpu.VMEM((4, 8, 128), f32),
            pltpu.VMEM((10, 8, 128), f32),
            dma((3,)), dma((3,)), dma((3,)), dma((3, 2, 2)), dma((3, 2, 2)), dma((3, 2)), dma((3, 2)),
            dma((3, 3)), dma((3, 3)), dma((3, 3)), dma((3, 3)), dma((3,)), dma((3,)), dma((10,)), dma((10,)),
        ],
        compiler_params=pltpu.CompilerParams(
            collective_id=1, has_side_effects=True, vmem_limit_bytes=32 * 1024 * 1024
        ),
        name="reduce_scatter",
    )(src.reshape(view), dst.reshape(view), out.reshape(view), bias.reshape(8, 128))
    index = lax.axis_index("region") * 8 + lax.axis_index("sub")
    part_bias = lax.dynamic_slice(o_bias.reshape(1024), (index * 8,), (8,))
    return o_src, o_dst, o_out, part_bias


def with_halo(cells, sides, width):
    for axis, dim in sides:
        count = lax.axis_size(axis)
        ends = count - 1
        head = lax.slice_in_dim(cells, 0, width, axis=dim)
        tail = lax.slice_in_dim(cells, cells.shape[dim] - width, cells.shape[dim], axis=dim)
        cells = jnp.concatenate(
            [
                lax.ppermute(tail, axis, [(i, (i + 1) % count) for i in range(ends)]),
                cells,
                lax.ppermute(head, axis, [((i + 1) % count, i) for i in range(ends)]),
            ],
            axis=dim,
        )
    return cells


def from_behind(block, axis, distance):
    devices = range(lax.axis_size(axis))
    route = [(i - distance, i) for i in devices if i - distance in devices]
    return lax.ppermute(block, axis, route)


def contract_rows(left, right):
    return lax.dot_general(
        left, right, (((0,), (0,)), ((), ())), preferred_element_type=jnp.float32
    )


def contract_cols(left, right):
    return lax.dot_general(
        left, right, (((1,), (1,)), ((), ())), preferred_element_type=jnp.float32
    )


def body(tokens, nodes, dests, token_count, w_src, w_dst, bias, w_out, cotangent):
    f32 = jnp.float32
    bf16 = jnp.bfloat16
    tok_rows = tokens.shape[0]
    node_rows = nodes.shape[0]
    hidden = w_src.shape[1]
    block_rows = min(512, tok_rows)
    region_index = lax.axis_index("region")
    sub_index = lax.axis_index("sub")
    sub_size = lax.axis_size("sub")
    node_proj = jnp.dot(nodes, w_dst, preferred_element_type=f32).astype(bf16)
    node_up = contract_cols(cotangent, w_out).astype(bf16)
    stacked = jnp.concatenate([node_proj, node_up], axis=0).reshape(1, 1, 2 * node_rows, hidden)
    padded = with_halo(stacked, (("region", 0), ("sub", 1)), 1)
    nearby = jnp.stack([padded[1, 1], padded[0, 1], padded[2, 1], padded[1, 0], padded[1, 2]])
    near_proj = nearby[:, :node_rows].reshape(5 * node_rows, hidden)
    near_up = nearby[:, node_rows:].reshape(5 * node_rows, hidden)
    owner_block = dests // node_rows
    local_row = dests % node_rows
    delta_row = owner_block // sub_size - region_index
    delta_col = owner_block % sub_size - sub_index
    slot_index = jnp.where(
        delta_row == -1,
        1,
        jnp.where(
            delta_row == 1, 2, jnp.where(delta_col == -1, 3, jnp.where(delta_col == 1, 4, 0))
        ),
    )
    near_index = slot_index * node_rows + local_row
    live_count = token_count[0]
    n_blocks = (live_count + block_rows - 1) // block_rows
    columns = jnp.arange(5 * node_rows, dtype=jnp.int32)

    def one_block(block_index, state_tuple):
        seg_fwd, seg_bwd, grad_src, grad_bias, token_grad = state_tuple
        start = block_index * block_rows
        x_block = lax.dynamic_slice_in_dim(tokens, start, block_rows, 0)
        near_block = lax.dynamic_slice_in_dim(near_index, start, block_rows, 0)
        row_ids = start + jnp.arange(block_rows, dtype=jnp.int32)
        live_mask = (row_ids < live_count).astype(f32)[:, None, None]
        token_proj = jnp.dot(x_block, w_src, preferred_element_type=f32)
        preact = token_proj[:, None, :] + jnp.take(near_proj, near_block, axis=0).astype(f32) + bias
        sigma = jax.nn.sigmoid(preact)
        edge_act = (preact * sigma * live_mask).astype(bf16)
        upstream = jnp.take(near_up, near_block, axis=0).astype(f32)
        edge_grad = (upstream * sigma * (1.0 + preact * (1.0 - sigma)) * live_mask).astype(bf16)
        onehot = (near_block.reshape(-1)[:, None] == columns[None, :]).astype(bf16)
        seg_fwd = seg_fwd + contract_rows(onehot, edge_act.reshape(-1, hidden))
        seg_bwd = seg_bwd + contract_rows(onehot, edge_grad.reshape(-1, hidden))
        grad_wide = edge_grad.astype(f32)
        token_back = jnp.sum(grad_wide, axis=1).astype(bf16)
        x_grad = contract_cols(token_back, w_src).astype(bf16)
        token_grad = lax.dynamic_update_slice_in_dim(token_grad, x_grad, start, 0)
        grad_src = grad_src + contract_rows(x_block, token_back)
        grad_bias = grad_bias + jnp.sum(grad_wide, axis=(0, 1))
        return (seg_fwd, seg_bwd, grad_src, grad_bias, token_grad)

    start_state = (
        jnp.zeros((5 * node_rows, hidden), f32),
        jnp.zeros((5 * node_rows, hidden), f32),
        jnp.zeros(w_src.shape, f32),
        jnp.zeros((hidden,), f32),
        jnp.zeros(tokens.shape, bf16),
    )
    seg_fwd, seg_bwd, grad_src, grad_bias, token_grad = lax.fori_loop(
        0, n_blocks, one_block, start_state
    )
    partials = jnp.concatenate(
        [
            seg_fwd.astype(bf16).reshape(5, node_rows, hidden),
            seg_bwd.astype(bf16).reshape(5, node_rows, hidden),
        ],
        axis=1,
    )
    summed = partials[0].astype(f32)
    for offset, slot_pick in ((1, 2), (-1, 1)):
        summed = summed + from_behind(partials[slot_pick], "region", offset).astype(f32)
    for offset, slot_pick in ((1, 4), (-1, 3)):
        summed = summed + from_behind(partials[slot_pick], "sub", offset).astype(f32)
    node_sum = summed[:node_rows].astype(bf16)
    node_back = summed[node_rows:].astype(bf16)
    updated = (nodes.astype(f32) + jnp.dot(node_sum, w_out, preferred_element_type=f32)).astype(
        bf16
    )
    node_grad = (cotangent.astype(f32) + contract_cols(node_back, w_dst)).astype(bf16)
    grad_dst = contract_rows(nodes, node_back)
    grad_out = contract_rows(node_sum, cotangent)
    part_src, part_dst, part_out, part_bias = reduce_scatter(
        grad_src.astype(bf16), grad_dst.astype(bf16), grad_out.astype(bf16), grad_bias
    )
    return (updated, token_grad, node_grad, part_src, part_dst, part_out, part_bias)


def solution(mesh):
    return jax.shard_map(
        body,
        mesh=mesh,
        in_specs=(
            P(("region", "sub"), None),
            P(("region", "sub"), None),
            P(("region", "sub"), None),
            P(("region", "sub")),
            P(),
            P(),
            P(),
            P(),
            P(("region", "sub"), None),
        ),
        out_specs=(
            P(("region", "sub"), None),
            P(("region", "sub"), None),
            P(("region", "sub"), None),
            P(("region", "sub"), None),
            P(("region", "sub"), None),
            P(("region", "sub"), None),
            P(("region", "sub")),
        ),
        check_vma=False,
    )
```

```python
import jax
import jax.numpy as jnp
from jax import lax
from jax.experimental import pallas as pl
from jax.experimental.pallas import tpu as pltpu
from jax.sharding import PartitionSpec as P

MESH = pl.DeviceIdType.MESH
F32, BF16 = jnp.float32, jnp.bfloat16
NODE = 160
NEAR = 5 * NODE
PAD = 896
CHUNK = 256
N_CHUNK = 4
DIMS = (0, 1, 2)
ORDERS = ((0, 2, 1), (2, 1, 0), (1, 0, 2))
BIAS_ORDER = (2, 1, 0)


def device_at(coords, core):
    return (coords[0] * 4 + coords[1], coords[2] * 2 + core)


def moved(coords, dim, value):
    return tuple(value if d == dim else c for d, c in enumerate(coords))


def pick(blocks):
    return tuple(blocks.get(d, slice(None)) for d in DIMS)


def partner(half, position):
    return position + 1 - 2 * (position % 2) if half == 0 else 3 - position


def dot(left, right):
    return jnp.dot(left, right, preferred_element_type=F32)


def dot_cols(left, right):
    return lax.dot_general(left, right, (((1,), (1,)), ((), ())), preferred_element_type=F32)


def dot_rows(left, right):
    return lax.dot_general(left, right, (((0,), (0,)), ((), ())), preferred_element_type=F32)


def lanes(start, size):
    return pl.ds(pl.multiple_of(start, 128), size)


def rows(start, size):
    return pl.ds(pl.multiple_of(start, 16), size)


def layer_kernel(
    tokens_hbm, nodes_hbm, dests_ref, count_ref, w_src_hbm, w_dst_hbm, bias_ref, w_out_hbm, cot_hbm,
    updated_ref, token_grad_hbm, node_grad_ref, o_src, o_dst, o_out, o_bias,
    tokens, nodes, w_src, w_dst, w_out, cot, tokens_t, nodes_t, ids, onehot, onehot_t, near, edges,
    back, part, rpart, nsum, nback, grads, stage, bias_sum,
    acc, pair, r1, r2, r3, r4, fin, fin_r, b_acc, b_r,
    in_sem, out_sem, near_s, near_v, part_s, part_v,
    pair_s, pair_v, s1, v1, s2, v2, s3, v3, s4, v4, fin_s, fin_v, b_s, b_v,
):
    region, sub = lax.axis_index("region"), lax.axis_index("sub")
    n_region, n_sub = 16, 8
    coords, core = (region // 4, region % 4, sub // 2), sub % 2
    twin = device_at(coords, 1 - core)
    ring = [
        [device_at(moved(coords, dim, (coords[dim] + hop) % 4), core) for hop in (1, 2, 3)]
        for dim in DIMS
    ]
    around = [
        (region, sub),
        ((region + n_region - 1) % n_region, sub),
        ((region + 1) % n_region, sub),
        (region, (sub + n_sub - 1) % n_sub),
        (region, (sub + 1) % n_sub),
    ]
    facing = (0, 2, 1, 4, 3)
    o_mats = (o_src, o_dst, o_out)
    outs = o_mats
    sends = []

    def remote(source, target, send, recv, device):
        return pltpu.make_async_remote_copy(
            src_ref=source, dst_ref=target, send_sem=send, recv_sem=recv,
            device_id=device, device_id_type=MESH,
        )

    def go(copy):
        copy.start()
        sends.append(copy)
        return copy

    loads = [
        pltpu.make_async_copy(source, target, in_sem.at[i])
        for i, (source, target) in enumerate((
            (nodes_hbm, nodes), (cot_hbm, cot), (w_dst_hbm, w_dst), (w_out_hbm, w_out),
            (w_src_hbm, w_src), (tokens_hbm, tokens),
        ))
    ]
    for load in loads:
        load.start()
    barrier = pltpu.get_barrier_semaphore()
    peers = [twin] + ring[0] + ring[1] + ring[2] + around[1:]
    for peer in peers:
        pl.semaphore_signal(barrier, inc=1, device_id=peer, device_id_type=MESH)

    def near_copy(c, slot):
        return remote(
            near.at[c, pl.ds(0, NODE)], near.at[c, pl.ds(slot * NODE, NODE)],
            near_s.at[c, slot - 1], near_v.at[c, slot - 1], around[facing[slot]],
        )

    def part_copy(c, slot):
        return remote(
            part.at[c, pl.ds(slot * NODE, NODE)], rpart.at[c, facing[slot] - 1],
            part_s.at[c, facing[slot] - 1], part_v.at[c, facing[slot] - 1], around[slot],
        )

    def pair_copy(m, c):
        if m == 2:
            return remote(
                grads.at[2, c, :, :, :, lanes((1 - core) * 512, 512)], pair.at[2, c],
                pair_s.at[2, c], pair_v.at[2, c], twin,
            )
        return remote(
            grads.at[m, :, :, :, :, lanes(c * CHUNK + (1 - core) * 128, 128)],
            pair.at[m, :, :, :, :, lanes(c * 128, 128)],
            pair_s.at[m, c], pair_v.at[m, c], twin,
        )

    for load in loads[:4]:
        load.wait()
    pl.semaphore_wait(barrier, len(peers))

    def project(c, carry):
        span = pl.ds(pl.multiple_of(c * CHUNK, CHUNK), CHUNK)
        near[c, :NODE, :CHUNK] = dot(nodes[...], w_dst[:, span]).astype(BF16)
        near[c, :NODE, CHUNK:] = dot_cols(cot[...], w_out[span, :]).astype(BF16)
        for slot in (1, 2, 3, 4):
            near_copy(c, slot).start()
        near[c, NEAR:, :] = jnp.zeros((PAD - NEAR, 2 * CHUNK), BF16)
        return carry

    lax.fori_loop(0, N_CHUNK, project, 0)

    live = lax.broadcasted_iota(jnp.int32, (2, 1024), 1) < count_ref[0]
    ids[...] = jnp.zeros((8, 1024), jnp.int32)
    ids[:2] = jnp.where(live, dests_ref[...], -1)
    ids_t = ids[...].T
    base = [(around[s][0] * n_sub + around[s][1]) * NODE for s in range(5)]

    def node_ids(shape, dim):
        place = lax.broadcasted_iota(jnp.int32, shape, dim)
        value = jnp.full(shape, -2, jnp.int32)
        for s in range(4, -1, -1):
            value = jnp.where(place < (s + 1) * NODE, place + (base[s] - s * NODE), value)
        return value

    across, down = node_ids((1, PAD), 1), node_ids((NEAR, 1), 0)
    for tb in range(4):
        for k in range(2):
            here = (tb * 2 + k) * 256
            onehot[here : here + 256, :] = jnp.where(
                ids_t[tb * 256 : tb * 256 + 256, k : k + 1] == across, 1.0, 0.0
            ).astype(BF16)
            onehot_t[:, here : here + 256] = jnp.where(
                down == ids[k : k + 1, tb * 256 : tb * 256 + 256], 1.0, 0.0
            ).astype(BF16)
    nodes_t[...] = nodes[...].T
    for load in loads[4:]:
        load.wait()

    def turn(i, carry):
        tokens_t[:, lanes(i * 256, 256)] = tokens[rows(i * 256, 256), :].T
        return carry

    lax.fori_loop(0, 4, turn, 0)
    bias_sum[...] = jnp.zeros((8, 1024), F32)

    def edge_chunk(c):
        span = pl.ds(pl.multiple_of(c * CHUNK, CHUNK), CHUNK)
        for slot in (1, 2, 3, 4):
            near_copy(c, slot).wait_recv()

        def token_block(tb, carry):
            here = rows(tb * 256, 256)
            plain = dot(tokens[here, :], w_src[:, span]) + bias_ref[:, span]
            total = jnp.zeros((256, CHUNK), F32)
            for k in range(2):
                there = rows((tb * 2 + k) * 256, 256)
                found = dot(onehot[there, :], near[c])
                preact = plain + found[:, :CHUNK]
                sigma = 0.5 * jnp.tanh(0.5 * preact) + 0.5
                act = preact * sigma
                grad = found[:, CHUNK:] * (sigma + act * (1.0 - sigma))
                edges[there, :CHUNK] = act.astype(BF16)
                edges[there, CHUNK:] = grad.astype(BF16)
                total = total + grad
            back[here, span] = total.astype(BF16)
            bias_sum[:, span] += jnp.sum(total.reshape(32, 8, CHUNK), axis=0)
            return carry

        lax.fori_loop(0, 4, token_block, 0)

        def scatter(i, carry):
            here = rows(i * 400, 400)
            part[c, here, :] = dot(onehot_t[here, :], edges[...]).astype(BF16)
            return carry

        lax.fori_loop(0, 2, scatter, 0)
        for slot in (1, 2, 3, 4):
            part_copy(c, slot).start()

        def source(z, carry):
            value = dot(tokens_t[rows(z * 256, 256), :], back[:, span])
            grads[0, z, :, :, :, span] = value.astype(BF16).reshape(4, 4, 16, CHUNK)
            return carry

        lax.fori_loop(0, 4, source, 0)
        pair_copy(0, c).start()

    def node_chunk(c):
        span = pl.ds(pl.multiple_of(c * CHUNK, CHUNK), CHUNK)
        total = part[c, :NODE].astype(F32)
        for slot in (1, 2, 3, 4):
            part_copy(c, facing[slot]).wait_recv()
            total = total + rpart[c, slot - 1].astype(F32)
        total = total.astype(BF16)
        nsum[:, span] = total[:, :CHUNK]
        nback[:, span] = total[:, CHUNK:]

        def weight(z, carry):
            value = dot(nodes_t[rows(z * 256, 256), :], nback[:, span])
            grads[1, z, :, :, :, span] = value.astype(BF16).reshape(4, 4, 16, CHUNK)
            return carry

        lax.fori_loop(0, 4, weight, 0)
        pair_copy(1, c).start()
        value = dot_rows(nsum[:, span], cot[...])
        grads[2, c] = value.astype(BF16).reshape(4, 4, 16, 1024)
        pair_copy(2, c).start()

    def chunk(c, carry):
        edge_chunk(c)

        @pl.when(c > 0)
        def _():
            node_chunk(c - 1)

        return carry

    lax.fori_loop(0, N_CHUNK, chunk, 0)

    cols = (pl.ds(0, 256), pl.ds(256, 256))

    def pair_add(m):
        for c in range(N_CHUNK):
            pair_copy(m, c).wait_recv()

        def add_rows(i, carry):
            z, y = i // 4, i % 4
            if m == 2:
                own = grads[m, z, y, :, :, lanes(core * 512, 512)]
                acc[m, z, y] = (own.astype(F32) + pair[m, z, y].astype(F32)).astype(BF16)
            else:
                for c in range(N_CHUNK):
                    own = grads[m, z, y, :, :, lanes(c * CHUNK + core * 128, 128)]
                    part_c = pl.ds(c * 128, 128)
                    other = pair[m, z, y, :, :, part_c]
                    acc[m, z, y, :, :, part_c] = (own.astype(F32) + other.astype(F32)).astype(BF16)
            return carry

        lax.fori_loop(0, 16, add_rows, 0)

    def step_one(m):
        dim = ORDERS[m][0]
        p = coords[dim]
        copies = []
        for half in range(2):
            q = partner(half, p)
            device = device_at(moved(coords, dim, q), core)
            for slot, block in ((1, partner(1 - half, q)), (0, q)):
                copies.append(go(remote(
                    acc.at[(m, *pick({dim: block}), slice(None), cols[half])],
                    r1.at[m, half, slot], s1.at[m, half, slot], v1.at[m, half, slot], device,
                )))
        return copies

    def add_in(m, blocks, half, value_ref):
        where = (m, *pick(blocks), slice(None), cols[half])
        acc[where] = (acc[where].astype(F32) + value_ref[...].astype(F32)).astype(BF16)

    def step_two(m, copies):
        dim = ORDERS[m][0]
        p = coords[dim]
        started = []
        for half in range(2):
            copies[2 * half].wait_recv()
            q = partner(1 - half, p)
            add_in(m, {dim: q}, half, r1.at[m, half, 1])
            started.append(go(remote(
                acc.at[(m, *pick({dim: q}), slice(None), cols[half])],
                r2.at[m, half], s2.at[m, half], v2.at[m, half],
                device_at(moved(coords, dim, q), core),
            )))
        for half in range(2):
            copies[2 * half + 1].wait_recv()
            add_in(m, {dim: p}, half, r1.at[m, half, 0])
        return started

    def step_three(m, copies):
        first, dim = ORDERS[m][0], ORDERS[m][1]
        p = coords[first]
        for half in range(2):
            copies[half].wait_recv()
            add_in(m, {first: p}, half, r2.at[m, half])
        started = []
        for hop in (2, 1, 3):
            block = (coords[dim] + hop) % 4
            started.append(go(remote(
                acc.at[(m, *pick({first: p, dim: block}))],
                r3.at[m, hop - 1], s3.at[m, hop - 1], v3.at[m, hop - 1], ring[dim][hop - 1],
            )))
        return started

    def step_four(m, copies):
        first, second, dim = ORDERS[m]
        for copy in copies:
            copy.wait_recv()
        where = (m, *pick({first: coords[first], second: coords[second]}))
        total = acc[where].astype(F32)
        for slot in range(3):
            total = total + r3[m, slot].astype(F32)
        acc[where] = total.astype(BF16)
        started = []
        for hop in (2, 1, 3):
            block = (coords[dim] + hop) % 4
            started.append(go(remote(
                acc.at[(m, *pick({first: coords[first], second: coords[second], dim: block}))],
                r4.at[m, hop - 1], s4.at[m, hop - 1], v4.at[m, hop - 1], ring[dim][hop - 1],
            )))
        return started

    def step_five(m, copies):
        for copy in copies:
            copy.wait_recv()
        total = acc[(m, *coords)].astype(F32)
        for slot in range(3):
            total = total + r4[m, slot].astype(F32)
        fin[m, 0] = total[:8]
        fin[m, 1] = total[8:]
        return go(remote(fin.at[m, 1 - core], fin_r.at[m], fin_s.at[m], fin_v.at[m], twin))

    def bias_send(stage):
        if stage == 3:
            return [go(remote(b_acc.at[3], b_r.at[9], b_s.at[9], b_v.at[9], twin))]
        started = []
        for hop in range(3):
            slot = 3 * stage + hop
            started.append(go(remote(
                b_acc.at[stage], b_r.at[slot], b_s.at[slot], b_v.at[slot],
                ring[BIAS_ORDER[stage]][hop],
            )))
        return started

    def bias_add(stage, copies):
        total = b_acc[stage]
        for copy in copies:
            copy.wait_recv()
        for slot in range(3 * stage, 3 * stage + len(copies)):
            total = total + b_r[slot]
        return total

    def token_grad_block(i):
        here = pl.ds(i * 256, 256)
        stage[here, :] = dot_cols(back[here, :], w_src[...]).astype(BF16)
        copy = pltpu.make_async_copy(stage.at[here], token_grad_hbm.at[here], out_sem.at[i])
        copy.start()
        return copy

    for i in range(8):
        b_acc[0, i : i + 1, :] = jnp.sum(bias_sum[:, i * 128 : i * 128 + 128], axis=0, keepdims=True)
    b_copies = bias_send(0)
    pair_add(0)
    src = step_one(0)
    written = [token_grad_block(0)]
    node_chunk(N_CHUNK - 1)
    src = step_two(0, src)
    b_acc[1] = bias_add(0, b_copies)
    b_copies = bias_send(1)
    pair_add(1)
    dst = step_one(1)
    pair_add(2)
    out = step_one(2)
    src = step_three(0, src)
    written.append(token_grad_block(1))
    b_acc[2] = bias_add(1, b_copies)
    b_copies = bias_send(2)
    src = step_four(0, src)
    dst = step_two(1, dst)
    out = step_two(2, out)
    written.append(token_grad_block(2))
    src = step_five(0, src)
    b_acc[3] = bias_add(2, b_copies)
    b_copies = bias_send(3)
    dst = step_three(1, dst)
    out = step_three(2, out)
    written.append(token_grad_block(3))
    dst = step_four(1, dst)
    out = step_four(2, out)
    updated_ref[...] = (nodes[...].astype(F32) + dot(nsum[...], w_out[...])).astype(BF16)
    node_grad_ref[...] = (cot[...].astype(F32) + dot_cols(nback[...], w_dst[...])).astype(BF16)
    dst = step_five(1, dst)
    out = step_five(2, out)
    o_bias[...] = bias_add(3, b_copies)
    for m, last in enumerate((src, dst, out)):
        last.wait_recv()
        if m == 2:
            outs[m][:, lanes(core * 512, 512)] = fin[m, core]
            outs[m][:, lanes((1 - core) * 512, 512)] = fin_r[m]
        else:
            for c in range(N_CHUNK):
                part_c = pl.ds(c * 128, 128)
                outs[m][:, lanes(c * CHUNK + core * 128, 128)] = fin[m, core, :, part_c]
                outs[m][:, lanes(c * CHUNK + (1 - core) * 128, 128)] = fin_r[m, :, part_c]
    for copy in written:
        copy.wait()
    for copy in sends:
        copy.wait_send()

    def settle(c, carry):
        for slot in (1, 2, 3, 4):
            near_copy(c, slot).wait_send()
            part_copy(c, slot).wait_send()
        for m in range(3):
            pair_copy(m, c).wait_send()
        return carry

    lax.fori_loop(0, N_CHUNK, settle, 0)


def body(tokens, nodes, dests, token_count, w_src, w_dst, bias, w_out, cotangent):
    dma = pltpu.SemaphoreType.DMA
    vmem = pl.BlockSpec(memory_space=pltpu.VMEM)
    smem = pl.BlockSpec(memory_space=pltpu.SMEM)
    hbm = pl.BlockSpec(memory_space=pl.ANY)
    slab = jax.ShapeDtypeStruct((8, 1024), F32)
    node_like = jax.ShapeDtypeStruct((NODE, 1024), BF16)
    whole = (1024, 1024)
    updated, token_grad, node_grad, o_src, o_dst, o_out, o_bias = pl.pallas_call(
        layer_kernel,
        out_shape=(
            node_like, jax.ShapeDtypeStruct(whole, BF16), node_like, slab, slab, slab,
            jax.ShapeDtypeStruct((8, 128), F32),
        ),
        in_specs=[hbm, hbm, vmem, smem, hbm, hbm, vmem, hbm, hbm],
        out_specs=[vmem, hbm, vmem, vmem, vmem, vmem, vmem],
        scratch_shapes=[
            pltpu.VMEM(whole, BF16), pltpu.VMEM((NODE, 1024), BF16), pltpu.VMEM(whole, BF16),
            pltpu.VMEM(whole, BF16), pltpu.VMEM(whole, BF16), pltpu.VMEM((NODE, 1024), BF16),
            pltpu.VMEM(whole, BF16), pltpu.VMEM((1024, NODE), BF16), pltpu.VMEM((8, 1024), jnp.int32),
            pltpu.VMEM((2048, PAD), BF16), pltpu.VMEM((NEAR, 2048), BF16),
            pltpu.VMEM((N_CHUNK, PAD, 2 * CHUNK), BF16), pltpu.VMEM((2048, 2 * CHUNK), BF16),
            pltpu.VMEM(whole, BF16), pltpu.VMEM((N_CHUNK, NEAR, 2 * CHUNK), BF16),
            pltpu.VMEM((N_CHUNK, 4, NODE, 2 * CHUNK), BF16), pltpu.VMEM((NODE, 1024), BF16),
            pltpu.VMEM((NODE, 1024), BF16), pltpu.VMEM((3, 4, 4, 4, 16, 1024), BF16),
            pltpu.VMEM(whole, BF16), pltpu.VMEM((8, 1024), F32),
            pltpu.VMEM((3, 4, 4, 4, 16, 512), BF16),
            pltpu.VMEM((3, 4, 4, 4, 16, 512), BF16),
            pltpu.VMEM((3, 2, 2, 4, 4, 16, 256), BF16),
            pltpu.VMEM((3, 2, 4, 4, 16, 256), BF16),
            pltpu.VMEM((3, 3, 4, 16, 512), BF16),
            pltpu.VMEM((3, 3, 16, 512), BF16),
            pltpu.VMEM((3, 2, 8, 512), F32),
            pltpu.VMEM((3, 8, 512), F32),
            pltpu.VMEM((4, 8, 128), F32),
            pltpu.VMEM((10, 8, 128), F32),
            dma((6,)), dma((4,)), dma((4, 4)), dma((4, 4)), dma((4, 4)), dma((4, 4)),
            dma((3, 4)), dma((3, 4)), dma((3, 2, 2)), dma((3, 2, 2)), dma((3, 2)), dma((3, 2)),
            dma((3, 3)), dma((3, 3)), dma((3, 3)), dma((3, 3)), dma((3,)), dma((3,)), dma((10,)), dma((10,)),
        ],
        compiler_params=pltpu.CompilerParams(
            collective_id=1, has_side_effects=True, vmem_limit_bytes=60 * 1024 * 1024
        ),
        name="layer",
    )(
        tokens, nodes, dests.T, token_count, w_src, w_dst, bias.reshape(1, 1024), w_out, cotangent,
    )
    index = lax.axis_index("region") * 8 + lax.axis_index("sub")
    part_bias = lax.dynamic_slice(o_bias.reshape(1024), (index * 8,), (8,))
    return updated, token_grad, node_grad, o_src, o_dst, o_out, part_bias


def solution(mesh):
    return jax.shard_map(
        body,
        mesh=mesh,
        in_specs=(
            P(("region", "sub"), None),
            P(("region", "sub"), None),
            P(("region", "sub"), None),
            P(("region", "sub")),
            P(),
            P(),
            P(),
            P(),
            P(("region", "sub"), None),
        ),
        out_specs=(
            P(("region", "sub"), None),
            P(("region", "sub"), None),
            P(("region", "sub"), None),
            P(("region", "sub"), None),
            P(("region", "sub"), None),
            P(("region", "sub"), None),
            P(("region", "sub")),
        ),
        check_vma=False,
    )
```

```python
import jax
import jax.numpy as jnp
from jax import lax
from jax.experimental import pallas as pl
from jax.experimental.pallas import tpu as pltpu
from jax.sharding import PartitionSpec as P

MESH = pl.DeviceIdType.MESH
F32, BF16 = jnp.float32, jnp.bfloat16
NODE = 160
NEAR = 5 * NODE
PAD = 896
CHUNK = 256
N_CHUNK = 4
DIMS = (0, 1, 2)
ORDERS = ((2, 0, 1), (0, 1, 2), (1, 2, 0))
BIAS_ORDER = (2, 1, 0)
HOPS = (2, 1, 3)


def device_at(coords, core):
    return (coords[0] * 4 + coords[1], coords[2] * 2 + core)


def moved(coords, dim, value):
    return tuple(value if d == dim else c for d, c in enumerate(coords))


def pick(blocks):
    return tuple(blocks.get(d, slice(None)) for d in DIMS)


def dot(left, right):
    return jnp.dot(left, right, preferred_element_type=F32)


def dot_cols(left, right):
    return lax.dot_general(left, right, (((1,), (1,)), ((), ())), preferred_element_type=F32)


def dot_rows(left, right):
    return lax.dot_general(left, right, (((0,), (0,)), ((), ())), preferred_element_type=F32)


def lanes(start, size):
    return pl.ds(pl.multiple_of(start, 128), size)


def rows(start, size):
    return pl.ds(pl.multiple_of(start, 16), size)


def layer_kernel(
    tokens_hbm, nodes_hbm, dests_ref, count_ref, w_src_hbm, w_dst_hbm, bias_ref, w_out_hbm, cot_hbm,
    updated_ref, token_grad_hbm, node_grad_ref, o_src, o_dst, o_out, o_bias,
    tokens, nodes, w_src, w_dst, w_out, cot, tokens_t, nodes_t, ids, onehot, onehot_t, near, edges,
    back, part, rpart, nsum, nback, grads, stage, bias_sum,
    acc, pair, r1, r2, r3, fin, fin_r, b_acc, b_r,
    in_sem, out_sem, near_s, near_v, part_s, part_v,
    pair_s, pair_v, s1, v1, s2, v2, s3, v3, fin_s, fin_v, b_s, b_v,
):
    region, sub = lax.axis_index("region"), lax.axis_index("sub")
    n_region, n_sub = 16, 8
    coords, core = (region // 4, region % 4, sub // 2), sub % 2
    twin = device_at(coords, 1 - core)
    ring = [
        [device_at(moved(coords, dim, (coords[dim] + hop) % 4), core) for hop in (1, 2, 3)]
        for dim in DIMS
    ]
    around = [
        (region, sub),
        ((region + n_region - 1) % n_region, sub),
        ((region + 1) % n_region, sub),
        (region, (sub + n_sub - 1) % n_sub),
        (region, (sub + 1) % n_sub),
    ]
    facing = (0, 2, 1, 4, 3)
    outs = (o_src, o_dst, o_out)
    sends = []

    def remote(source, target, send, recv, device):
        return pltpu.make_async_remote_copy(
            src_ref=source, dst_ref=target, send_sem=send, recv_sem=recv,
            device_id=device, device_id_type=MESH,
        )

    def go(copy):
        copy.start()
        sends.append(copy)
        return copy

    loads = [
        pltpu.make_async_copy(source, target, in_sem.at[i])
        for i, (source, target) in enumerate((
            (nodes_hbm, nodes), (cot_hbm, cot), (w_dst_hbm, w_dst), (w_out_hbm, w_out),
            (w_src_hbm, w_src), (tokens_hbm, tokens),
        ))
    ]
    for load in loads:
        load.start()
    barrier = pltpu.get_barrier_semaphore()
    peers = [twin] + ring[0] + ring[1] + ring[2] + around[1:]
    for peer in peers:
        pl.semaphore_signal(barrier, inc=1, device_id=peer, device_id_type=MESH)

    def near_copy(c, slot):
        return remote(
            near.at[c, pl.ds(0, NODE)], near.at[c, pl.ds(slot * NODE, NODE)],
            near_s.at[c, slot - 1], near_v.at[c, slot - 1], around[facing[slot]],
        )

    def part_copy(c, slot):
        return remote(
            part.at[c, pl.ds(slot * NODE, NODE)], rpart.at[c, facing[slot] - 1],
            part_s.at[c, facing[slot] - 1], part_v.at[c, facing[slot] - 1], around[slot],
        )

    def pair_copy(m, c):
        if m == 2:
            return remote(
                grads.at[2, c, :, :, :, lanes((1 - core) * 512, 512)], pair.at[2, c],
                pair_s.at[2, c], pair_v.at[2, c], twin,
            )
        return remote(
            grads.at[m, :, :, :, :, lanes(c * CHUNK + (1 - core) * 128, 128)],
            pair.at[m, :, :, :, :, lanes(c * 128, 128)],
            pair_s.at[m, c], pair_v.at[m, c], twin,
        )

    live = lax.broadcasted_iota(jnp.int32, (2, 1024), 1) < count_ref[...]
    ids[...] = jnp.zeros((8, 1024), jnp.int32)
    ids[:2] = jnp.where(live, dests_ref[...], -1)
    ids_t = ids[...].T
    base = [(around[s][0] * n_sub + around[s][1]) * NODE for s in range(5)]

    def node_ids(shape, dim):
        place = lax.broadcasted_iota(jnp.int32, shape, dim)
        value = jnp.full(shape, -2, jnp.int32)
        for s in range(4, -1, -1):
            value = jnp.where(place < (s + 1) * NODE, place + (base[s] - s * NODE), value)
        return value

    across, down = node_ids((1, PAD), 1), node_ids((NEAR, 1), 0)
    for tb in range(4):
        for k in range(2):
            here = (tb * 2 + k) * 256
            onehot[here : here + 256, :] = jnp.where(
                ids_t[tb * 256 : tb * 256 + 256, k : k + 1] == across, 1.0, 0.0
            ).astype(BF16)
            onehot_t[:, here : here + 256] = jnp.where(
                down == ids[k : k + 1, tb * 256 : tb * 256 + 256], 1.0, 0.0
            ).astype(BF16)

    for load in loads[:4]:
        load.wait()
    pl.semaphore_wait(barrier, len(peers))

    def project(c, carry):
        span = pl.ds(pl.multiple_of(c * CHUNK, CHUNK), CHUNK)
        near[c, :NODE, :CHUNK] = dot(nodes[...], w_dst[:, span]).astype(BF16)
        near[c, :NODE, CHUNK:] = dot_cols(cot[...], w_out[span, :]).astype(BF16)
        for slot in (1, 2, 3, 4):
            near_copy(c, slot).start()
        near[c, NEAR:, :] = jnp.zeros((PAD - NEAR, 2 * CHUNK), BF16)
        return carry

    lax.fori_loop(0, N_CHUNK, project, 0)

    nodes_t[...] = nodes[...].T
    for load in loads[4:]:
        load.wait()

    def turn(i, carry):
        tokens_t[:, lanes(i * 256, 256)] = tokens[rows(i * 256, 256), :].T
        return carry

    lax.fori_loop(0, 4, turn, 0)
    bias_sum[...] = jnp.zeros((8, 1024), F32)

    def edge_chunk(c):
        span = pl.ds(pl.multiple_of(c * CHUNK, CHUNK), CHUNK)
        for slot in (1, 2, 3, 4):
            near_copy(c, slot).wait_recv()

        def token_block(tb, carry):
            here = rows(tb * 256, 256)
            plain = dot(tokens[here, :], w_src[:, span]) + bias_ref[:, span]
            total = jnp.zeros((256, CHUNK), F32)
            for k in range(2):
                there = rows((tb * 2 + k) * 256, 256)
                found = dot(onehot[there, :], near[c])
                preact = plain + found[:, :CHUNK]
                sigma = 0.5 * jnp.tanh(0.5 * preact) + 0.5
                act = preact * sigma
                grad = found[:, CHUNK:] * (sigma + act * (1.0 - sigma))
                edges[there, :CHUNK] = act.astype(BF16)
                edges[there, CHUNK:] = grad.astype(BF16)
                total = total + grad
            back[here, span] = total.astype(BF16)
            bias_sum[:, span] += jnp.sum(total.reshape(32, 8, CHUNK), axis=0)
            return carry

        lax.fori_loop(0, 4, token_block, 0, unroll=2)

        part[c] = dot(onehot_t[...], edges[...]).astype(BF16)
        for slot in (1, 2, 3, 4):
            part_copy(c, slot).start()

        value = dot(tokens_t[...], back[:, span])
        grads[0, :, :, :, :, span] = value.astype(BF16).reshape(4, 4, 4, 16, CHUNK)
        pair_copy(0, c).start()

    def node_chunk(c):
        span = pl.ds(pl.multiple_of(c * CHUNK, CHUNK), CHUNK)
        total = part[c, :NODE].astype(F32)
        for slot in (1, 2, 3, 4):
            part_copy(c, facing[slot]).wait_recv()
            total = total + rpart[c, slot - 1].astype(F32)
        total = total.astype(BF16)
        nsum[:, span] = total[:, :CHUNK]
        nback[:, span] = total[:, CHUNK:]

        value = dot(nodes_t[...], nback[:, span])
        grads[1, :, :, :, :, span] = value.astype(BF16).reshape(4, 4, 4, 16, CHUNK)
        pair_copy(1, c).start()
        value = dot_rows(nsum[:, span], cot[...])
        grads[2, c] = value.astype(BF16).reshape(4, 4, 16, 1024)
        pair_copy(2, c).start()

    def pair_add(m, c):
        pair_copy(m, c).wait_recv()
        if m == 2:
            own = grads[2, c, :, :, :, lanes(core * 512, 512)].astype(F32)
            acc[2, c] = (own + pair[2, c].astype(F32)).astype(BF16)
            return
        here = lanes(c * 128, 128)
        own = grads[m, :, :, :, :, lanes(c * CHUNK + core * 128, 128)].astype(F32)
        acc[m, :, :, :, :, here] = (own + pair[m, :, :, :, :, here].astype(F32)).astype(BF16)

    def first_copy(m, c, hop):
        dim = ORDERS[m][0]
        block = (coords[dim] + hop) % 4
        if m == 2:
            source, target = acc.at[2, c, block], r1.at[2, hop - 1, c]
        else:
            here = lanes(c * 128, 128)
            source = acc.at[(m, *pick({dim: block}), slice(None), here)]
            target = r1.at[m, hop - 1, :, :, :, here]
        return remote(source, target, s1.at[m, c, hop - 1], v1.at[m, c, hop - 1], ring[dim][hop - 1])

    def second_copy(m, c, hop):
        done, dim = ORDERS[m][:2]
        block = (coords[dim] + hop) % 4
        if m == 2:
            source, target = acc.at[2, c, coords[done], block], r2.at[2, hop - 1, c]
        else:
            here = lanes(c * 128, 128)
            source = acc.at[(m, *pick({done: coords[done], dim: block}), slice(None), here)]
            target = r2.at[m, hop - 1, :, :, here]
        return remote(source, target, s2.at[m, c, hop - 1], v2.at[m, c, hop - 1], ring[dim][hop - 1])

    def third_copy(m, hop):
        one, two, dim = ORDERS[m]
        block = (coords[dim] + hop) % 4
        source = acc.at[(m, *pick({one: coords[one], two: coords[two], dim: block}))]
        return remote(source, r3.at[m, hop - 1], s3.at[m, hop - 1], v3.at[m, hop - 1], ring[dim][hop - 1])

    def first_send(m, c):
        pair_add(m, c)
        for hop in HOPS:
            first_copy(m, c, hop).start()

    def second_send(m, c):
        dim = ORDERS[m][0]
        for hop in HOPS:
            first_copy(m, c, hop).wait_recv()
        if m == 2:
            total = acc[2, c, coords[dim]].astype(F32)
            for slot in range(3):
                total = total + r1[2, slot, c].astype(F32)
            acc[2, c, coords[dim]] = total.astype(BF16)
        else:
            here = lanes(c * 128, 128)
            where = (m, *pick({dim: coords[dim]}), slice(None), here)
            total = acc[where].astype(F32)
            for slot in range(3):
                total = total + r1[m, slot, :, :, :, here].astype(F32)
            acc[where] = total.astype(BF16)
        for hop in HOPS:
            second_copy(m, c, hop).start()

    def second_add(m, c):
        one, two = ORDERS[m][:2]
        for hop in HOPS:
            second_copy(m, c, hop).wait_recv()
        if m == 2:
            where = (2, c, coords[one], coords[two])
            total = acc[where].astype(F32)
            for slot in range(3):
                total = total + r2[2, slot, c].astype(F32)
        else:
            here = lanes(c * 128, 128)
            where = (m, *pick({one: coords[one], two: coords[two]}), slice(None), here)
            total = acc[where].astype(F32)
            for slot in range(3):
                total = total + r2[m, slot, :, :, here].astype(F32)
        acc[where] = total.astype(BF16)

    def third_send(m):
        for hop in HOPS:
            third_copy(m, hop).start()

    def last_send(m):
        for hop in HOPS:
            third_copy(m, hop).wait_recv()
        total = acc[(m, *coords)].astype(F32)
        for slot in range(3):
            total = total + r3[m, slot].astype(F32)
        fin[m, 0] = total[:8]
        fin[m, 1] = total[8:]
        last_copy(m).start()

    def last_copy(m):
        return remote(fin.at[m, 1 - core], fin_r.at[m], fin_s.at[m], fin_v.at[m], twin)

    def chunk(c, carry):
        edge_chunk(c)

        @pl.when(c > 0)
        def _():
            node_chunk(c - 1)
            first_send(0, c - 1)

        @pl.when(c > 1)
        def _():
            first_send(1, c - 2)
            first_send(2, c - 2)
            second_send(0, c - 2)

        @pl.when(c > 2)
        def _():
            second_send(1, c - 3)
            second_send(2, c - 3)
            second_add(0, c - 3)

        return carry

    lax.fori_loop(0, N_CHUNK, chunk, 0)

    def bias_send(stage):
        if stage == 3:
            return [go(remote(b_acc.at[3], b_r.at[9], b_s.at[9], b_v.at[9], twin))]
        started = []
        for hop in range(3):
            slot = 3 * stage + hop
            started.append(go(remote(
                b_acc.at[stage], b_r.at[slot], b_s.at[slot], b_v.at[slot],
                ring[BIAS_ORDER[stage]][hop],
            )))
        return started

    def bias_add(stage, copies):
        total = b_acc[stage]
        for copy in copies:
            copy.wait_recv()
        for slot in range(3 * stage, 3 * stage + len(copies)):
            total = total + b_r[slot]
        return total

    def token_grad_block(i):
        here = pl.ds(i * 256, 256)
        stage[here, :] = dot_cols(back[here, :], w_src[...]).astype(BF16)
        copy = pltpu.make_async_copy(stage.at[here], token_grad_hbm.at[here], out_sem.at[i])
        copy.start()
        return copy

    for i in range(8):
        b_acc[0, i : i + 1, :] = jnp.sum(bias_sum[:, i * 128 : i * 128 + 128], axis=0, keepdims=True)
    b_copies = bias_send(0)
    first_send(0, 3)
    first_send(1, 2)
    first_send(2, 2)
    second_send(0, 2)
    second_send(1, 1)
    second_send(2, 1)
    written = [token_grad_block(0)]
    node_chunk(3)
    b_acc[1] = bias_add(0, b_copies)
    b_copies = bias_send(1)
    written.append(token_grad_block(1))
    first_send(1, 3)
    first_send(2, 3)
    second_send(0, 3)
    second_send(1, 2)
    second_send(2, 2)
    b_acc[2] = bias_add(1, b_copies)
    b_copies = bias_send(2)
    second_add(0, 1)
    second_add(0, 2)
    second_add(1, 0)
    second_add(2, 0)
    written.append(token_grad_block(2))
    second_send(1, 3)
    second_send(2, 3)
    second_add(0, 3)
    third_send(0)
    b_acc[3] = bias_add(2, b_copies)
    b_copies = bias_send(3)
    second_add(1, 1)
    second_add(2, 1)
    second_add(1, 2)
    second_add(2, 2)
    written.append(token_grad_block(3))
    second_add(1, 3)
    third_send(1)
    second_add(2, 3)
    third_send(2)
    updated_ref[...] = (nodes[...].astype(F32) + dot(nsum[...], w_out[...])).astype(BF16)
    node_grad_ref[...] = (cot[...].astype(F32) + dot_cols(nback[...], w_dst[...])).astype(BF16)
    o_bias[...] = bias_add(3, b_copies)
    for m in range(3):
        last_send(m)
    for m in range(3):
        last_copy(m).wait_recv()
        if m == 2:
            outs[m][:, lanes(core * 512, 512)] = fin[m, core]
            outs[m][:, lanes((1 - core) * 512, 512)] = fin_r[m]
        else:
            for c in range(N_CHUNK):
                part_c = pl.ds(c * 128, 128)
                outs[m][:, lanes(c * CHUNK + core * 128, 128)] = fin[m, core, :, part_c]
                outs[m][:, lanes(c * CHUNK + (1 - core) * 128, 128)] = fin_r[m, :, part_c]
    for copy in written:
        copy.wait()
    for copy in sends:
        copy.wait_send()

    def settle(c, carry):
        for slot in (1, 2, 3, 4):
            near_copy(c, slot).wait_send()
            part_copy(c, slot).wait_send()
        for m in range(3):
            pair_copy(m, c).wait_send()
            for hop in HOPS:
                first_copy(m, c, hop).wait_send()
                second_copy(m, c, hop).wait_send()
        return carry

    lax.fori_loop(0, N_CHUNK, settle, 0)
    for m in range(3):
        last_copy(m).wait_send()
        for hop in HOPS:
            third_copy(m, hop).wait_send()


def finish_kernel(*refs):
    ins, b_ref, outs, o_ref, sems = refs[:6], refs[6], refs[7:13], refs[13], refs[14]
    copies = []
    for i, (source, target) in enumerate(zip(ins, outs)):
        pieces = 4 if source.shape[0] == 1024 else 1
        size = source.shape[0] // pieces
        for piece in range(pieces):
            here = pl.ds(piece * size, size)
            copies.append(pltpu.make_async_copy(source.at[here], target.at[here], sems.at[i, piece]))
    for copy in copies:
        copy.start()
    index = lax.axis_index("region") * 8 + lax.axis_index("sub")
    turned = pltpu.roll(b_ref[...], (128 - index % 16 * 8) % 128, axis=1)
    own = lax.broadcasted_iota(jnp.int32, (8, 128), 0) == index // 16
    o_ref[...] = jnp.sum(jnp.where(own, turned, 0.0), axis=0, keepdims=True)[:, :8]
    for copy in copies:
        copy.wait()


def finish(arrays, bias_sums):
    vmem = pl.BlockSpec(memory_space=pltpu.VMEM)
    hbm = pl.BlockSpec(memory_space=pl.ANY)
    *results, part_bias = pl.pallas_call(
        finish_kernel,
        out_shape=(
            *[jax.ShapeDtypeStruct(a.shape, a.dtype) for a in arrays],
            jax.ShapeDtypeStruct((1, 8), F32),
        ),
        in_specs=[hbm] * 6 + [vmem],
        out_specs=[hbm] * 6 + [vmem],
        scratch_shapes=[pltpu.SemaphoreType.DMA((6, 4))],
        compiler_params=pltpu.CompilerParams(vmem_limit_bytes=60 * 1024 * 1024),
        name="finish",
    )(*arrays, bias_sums)
    return (*results, part_bias.reshape(8))


def body(tokens, nodes, dests, token_count, w_src, w_dst, bias, w_out, cotangent):
    dma = pltpu.SemaphoreType.DMA
    vmem = pl.BlockSpec(memory_space=pltpu.VMEM)
    hbm = pl.BlockSpec(memory_space=pl.ANY)
    slab = jax.ShapeDtypeStruct((8, 1024), F32)
    node_like = jax.ShapeDtypeStruct((NODE, 1024), BF16)
    whole = (1024, 1024)
    updated, token_grad, node_grad, o_src, o_dst, o_out, o_bias = pl.pallas_call(
        layer_kernel,
        out_shape=(
            node_like, jax.ShapeDtypeStruct(whole, BF16), node_like, slab, slab, slab,
            jax.ShapeDtypeStruct((8, 128), F32),
        ),
        in_specs=[hbm, hbm, vmem, vmem, hbm, hbm, vmem, hbm, hbm],
        out_specs=[vmem, hbm, vmem, vmem, vmem, vmem, vmem],
        scratch_shapes=[
            pltpu.VMEM(whole, BF16), pltpu.VMEM((NODE, 1024), BF16), pltpu.VMEM(whole, BF16),
            pltpu.VMEM(whole, BF16), pltpu.VMEM(whole, BF16), pltpu.VMEM((NODE, 1024), BF16),
            pltpu.VMEM(whole, BF16), pltpu.VMEM((1024, NODE), BF16), pltpu.VMEM((8, 1024), jnp.int32),
            pltpu.VMEM((2048, PAD), BF16), pltpu.VMEM((NEAR, 2048), BF16),
            pltpu.VMEM((N_CHUNK, PAD, 2 * CHUNK), BF16), pltpu.VMEM((2048, 2 * CHUNK), BF16),
            pltpu.VMEM(whole, BF16), pltpu.VMEM((N_CHUNK, NEAR, 2 * CHUNK), BF16),
            pltpu.VMEM((N_CHUNK, 4, NODE, 2 * CHUNK), BF16), pltpu.VMEM((NODE, 1024), BF16),
            pltpu.VMEM((NODE, 1024), BF16), pltpu.VMEM((3, 4, 4, 4, 16, 1024), BF16),
            pltpu.VMEM(whole, BF16), pltpu.VMEM((8, 1024), F32),
            pltpu.VMEM((3, 4, 4, 4, 16, 512), BF16),
            pltpu.VMEM((3, 4, 4, 4, 16, 512), BF16),
            pltpu.VMEM((3, 3, 4, 4, 16, 512), BF16),
            pltpu.VMEM((3, 3, 4, 16, 512), BF16),
            pltpu.VMEM((3, 3, 16, 512), BF16),
            pltpu.VMEM((3, 2, 8, 512), F32),
            pltpu.VMEM((3, 8, 512), F32),
            pltpu.VMEM((4, 8, 128), F32),
            pltpu.VMEM((10, 8, 128), F32),
            dma((6,)), dma((4,)), dma((4, 4)), dma((4, 4)), dma((4, 4)), dma((4, 4)),
            dma((3, 4)), dma((3, 4)), dma((3, 4, 3)), dma((3, 4, 3)), dma((3, 4, 3)), dma((3, 4, 3)),
            dma((3, 3)), dma((3, 3)), dma((3,)), dma((3,)), dma((10,)), dma((10,)),
        ],
        compiler_params=pltpu.CompilerParams(
            collective_id=1, has_side_effects=True, vmem_limit_bytes=60 * 1024 * 1024
        ),
        name="layer",
    )(
        tokens, nodes, dests.T, token_count.reshape(1, 1), w_src, w_dst, bias.reshape(1, 1024), w_out, cotangent,
    )
    return finish((updated, token_grad, node_grad, o_src, o_dst, o_out), o_bias)


def solution(mesh):
    return jax.shard_map(
        body,
        mesh=mesh,
        in_specs=(
            P(("region", "sub"), None),
            P(("region", "sub"), None),
            P(("region", "sub"), None),
            P(("region", "sub")),
            P(),
            P(),
            P(),
            P(),
            P(("region", "sub"), None),
        ),
        out_specs=(
            P(("region", "sub"), None),
            P(("region", "sub"), None),
            P(("region", "sub"), None),
            P(("region", "sub"), None),
            P(("region", "sub"), None),
            P(("region", "sub"), None),
            P(("region", "sub")),
        ),
        check_vma=False,
    )
```

```python
import jax
import jax.numpy as jnp
from jax import lax
from jax.experimental import pallas as pl
from jax.experimental.pallas import tpu as pltpu
from jax.sharding import PartitionSpec as P

MESH = pl.DeviceIdType.MESH
F32, BF16 = jnp.float32, jnp.bfloat16
NODE = 160
NEAR = 5 * NODE
PAD = 896
CHUNK = 256
N_CHUNK = 4
DIMS = (0, 1, 2)
ORDERS = ((2, 0, 1), (0, 1, 2), (1, 2, 0))
BIAS_ORDER = (2, 1, 0)
HOPS = (2, 1, 3)


def device_at(coords, core):
    return (coords[0] * 4 + coords[1], coords[2] * 2 + core)


def moved(coords, dim, value):
    return tuple(value if d == dim else c for d, c in enumerate(coords))


def pick(blocks):
    return tuple(blocks.get(d, slice(None)) for d in DIMS)


def dot(left, right):
    return jnp.dot(left, right, preferred_element_type=F32)


def dot_cols(left, right):
    return lax.dot_general(left, right, (((1,), (1,)), ((), ())), preferred_element_type=F32)


def dot_rows(left, right):
    return lax.dot_general(left, right, (((0,), (0,)), ((), ())), preferred_element_type=F32)


def lanes(start, size):
    return pl.ds(pl.multiple_of(start, 128), size)


def rows(start, size):
    return pl.ds(pl.multiple_of(start, 16), size)


def layer_kernel(
    tokens_hbm, nodes_hbm, dests_ref, count_ref, w_src_hbm, w_dst_hbm, bias_ref, w_out_hbm, cot_hbm,
    updated_ref, token_grad_hbm, node_grad_ref, o_src, o_dst, o_out, o_bias,
    tokens, nodes, w_src, w_dst, w_out, cot, tokens_t, nodes_t, ids, onehot, onehot_t, near, edges,
    back, part, rpart, nsum, nback, grads, stage, bias_sum,
    acc, pair, r1, r2, r3, fin, fin_r, b_acc, b_r,
    in_sem, out_sem, near_s, near_v, part_s, part_v,
    pair_s, pair_v, s1, v1, s2, v2, s3, v3, fin_s, fin_v, b_s, b_v,
):
    region, sub = lax.axis_index("region"), lax.axis_index("sub")
    n_region, n_sub = 16, 8
    coords, core = (region // 4, region % 4, sub // 2), sub % 2
    twin = device_at(coords, 1 - core)
    ring = [
        [device_at(moved(coords, dim, (coords[dim] + hop) % 4), core) for hop in (1, 2, 3)]
        for dim in DIMS
    ]
    around = [
        (region, sub),
        ((region + n_region - 1) % n_region, sub),
        ((region + 1) % n_region, sub),
        (region, (sub + n_sub - 1) % n_sub),
        (region, (sub + 1) % n_sub),
    ]
    facing = (0, 2, 1, 4, 3)
    outs = (o_src, o_dst, o_out)
    sends = []

    def remote(source, target, send, recv, device):
        return pltpu.make_async_remote_copy(
            src_ref=source, dst_ref=target, send_sem=send, recv_sem=recv,
            device_id=device, device_id_type=MESH,
        )

    def go(copy):
        copy.start()
        sends.append(copy)
        return copy

    loads = [
        pltpu.make_async_copy(source, target, in_sem.at[i])
        for i, (source, target) in enumerate((
            (nodes_hbm, nodes), (cot_hbm, cot), (w_dst_hbm, w_dst), (w_out_hbm, w_out),
            (w_src_hbm, w_src), (tokens_hbm, tokens),
        ))
    ]
    for load in loads:
        load.start()
    barrier = pltpu.get_barrier_semaphore()
    peers = [twin] + ring[0] + ring[1] + ring[2] + around[1:]
    for peer in peers:
        pl.semaphore_signal(barrier, inc=1, device_id=peer, device_id_type=MESH)

    def near_copy(c, slot):
        return remote(
            near.at[c, pl.ds(0, NODE)], near.at[c, pl.ds(slot * NODE, NODE)],
            near_s.at[c, slot - 1], near_v.at[c, slot - 1], around[facing[slot]],
        )

    def part_copy(c, slot):
        return remote(
            part.at[c, pl.ds(slot * NODE, NODE)], rpart.at[c, facing[slot] - 1],
            part_s.at[c, facing[slot] - 1], part_v.at[c, facing[slot] - 1], around[slot],
        )

    def pair_copy(m, c):
        if m == 2:
            return remote(
                grads.at[2, c, :, :, :, lanes((1 - core) * 512, 512)], pair.at[2, c],
                pair_s.at[2, c], pair_v.at[2, c], twin,
            )
        return remote(
            grads.at[m, :, :, :, :, lanes(c * CHUNK + (1 - core) * 128, 128)],
            pair.at[m, :, :, :, :, lanes(c * 128, 128)],
            pair_s.at[m, c], pair_v.at[m, c], twin,
        )

    live = lax.broadcasted_iota(jnp.int32, (2, 1024), 1) < count_ref[...]
    ids[...] = jnp.zeros((8, 1024), jnp.int32)
    ids[:2] = jnp.where(live, dests_ref[...], -1)
    ids_t = ids[...].T
    base = [(around[s][0] * n_sub + around[s][1]) * NODE for s in range(5)]

    def node_ids(shape, dim):
        place = lax.broadcasted_iota(jnp.int32, shape, dim)
        value = jnp.full(shape, -2, jnp.int32)
        for s in range(4, -1, -1):
            value = jnp.where(place < (s + 1) * NODE, place + (base[s] - s * NODE), value)
        return value

    across, down = node_ids((1, PAD), 1), node_ids((NEAR, 1), 0)
    for tb in range(4):
        for k in range(2):
            here = (tb * 2 + k) * 256
            onehot[here : here + 256, :] = jnp.where(
                ids_t[tb * 256 : tb * 256 + 256, k : k + 1] == across, 1.0, 0.0
            ).astype(BF16)
            onehot_t[:, here : here + 256] = jnp.where(
                down == ids[k : k + 1, tb * 256 : tb * 256 + 256], 1.0, 0.0
            ).astype(BF16)

    for load in loads[:4]:
        load.wait()
    pl.semaphore_wait(barrier, len(peers))

    def project(c, carry):
        span = pl.ds(pl.multiple_of(c * CHUNK, CHUNK), CHUNK)
        near[c, :NODE, :CHUNK] = dot(nodes[...], w_dst[:, span]).astype(BF16)
        near[c, :NODE, CHUNK:] = dot_cols(cot[...], w_out[span, :]).astype(BF16)
        for slot in (1, 2, 3, 4):
            near_copy(c, slot).start()
        near[c, NEAR:, :] = jnp.zeros((PAD - NEAR, 2 * CHUNK), BF16)
        return carry

    lax.fori_loop(0, N_CHUNK, project, 0)

    nodes_t[...] = nodes[...].T
    for load in loads[4:]:
        load.wait()

    def turn(i, carry):
        tokens_t[:, lanes(i * 256, 256)] = tokens[rows(i * 256, 256), :].T
        return carry

    lax.fori_loop(0, 4, turn, 0)
    bias_sum[...] = jnp.zeros((8, 1024), F32)

    def edge_chunk(c):
        span = pl.ds(pl.multiple_of(c * CHUNK, CHUNK), CHUNK)
        for slot in (1, 2, 3, 4):
            near_copy(c, slot).wait_recv()

        def token_block(tb, carry):
            here = rows(tb * 256, 256)
            plain = dot(tokens[here, :], w_src[:, span]) + bias_ref[:, span]
            total = jnp.zeros((256, CHUNK), F32)
            for k in range(2):
                there = rows((tb * 2 + k) * 256, 256)
                found = dot(onehot[there, :], near[c])
                preact = plain + found[:, :CHUNK]
                sigma = 0.5 * jnp.tanh(0.5 * preact) + 0.5
                act = preact * sigma
                grad = found[:, CHUNK:] * (sigma + act * (1.0 - sigma))
                edges[there, :CHUNK] = act.astype(BF16)
                edges[there, CHUNK:] = grad.astype(BF16)
                total = total + grad
            back[here, span] = total.astype(BF16)
            bias_sum[:, span] += jnp.sum(total.reshape(32, 8, CHUNK), axis=0)
            return carry

        lax.fori_loop(0, 4, token_block, 0, unroll=2)

        part[c] = dot(onehot_t[...], edges[...]).astype(BF16)
        for slot in (1, 2, 3, 4):
            part_copy(c, slot).start()

        value = dot(tokens_t[...], back[:, span])
        grads[0, :, :, :, :, span] = value.astype(BF16).reshape(4, 4, 4, 16, CHUNK)
        pair_copy(0, c).start()

    def node_chunk(c):
        span = pl.ds(pl.multiple_of(c * CHUNK, CHUNK), CHUNK)
        total = part[c, :NODE].astype(F32)
        for slot in (1, 2, 3, 4):
            part_copy(c, facing[slot]).wait_recv()
            total = total + rpart[c, slot - 1].astype(F32)
        total = total.astype(BF16)
        nsum[:, span] = total[:, :CHUNK]
        nback[:, span] = total[:, CHUNK:]

        value = dot(nodes_t[...], nback[:, span])
        grads[1, :, :, :, :, span] = value.astype(BF16).reshape(4, 4, 4, 16, CHUNK)
        pair_copy(1, c).start()
        value = dot_rows(nsum[:, span], cot[...])
        grads[2, c] = value.astype(BF16).reshape(4, 4, 16, 1024)
        pair_copy(2, c).start()

    def pair_add(m, c):
        pair_copy(m, c).wait_recv()
        if m == 2:
            own = grads[2, c, :, :, :, lanes(core * 512, 512)].astype(F32)
            acc[2, c] = (own + pair[2, c].astype(F32)).astype(BF16)
            return
        here = lanes(c * 128, 128)
        own = grads[m, :, :, :, :, lanes(c * CHUNK + core * 128, 128)].astype(F32)
        acc[m, :, :, :, :, here] = (own + pair[m, :, :, :, :, here].astype(F32)).astype(BF16)

    def first_copy(m, c, hop):
        dim = ORDERS[m][0]
        block = (coords[dim] + hop) % 4
        if m == 2:
            source, target = acc.at[2, c, block], r1.at[2, hop - 1, c]
        else:
            here = lanes(c * 128, 128)
            source = acc.at[(m, *pick({dim: block}), slice(None), here)]
            target = r1.at[m, hop - 1, :, :, :, here]
        return remote(source, target, s1.at[m, c, hop - 1], v1.at[m, c, hop - 1], ring[dim][hop - 1])

    def second_copy(m, c, hop):
        done, dim = ORDERS[m][:2]
        block = (coords[dim] + hop) % 4
        if m == 2:
            source, target = acc.at[2, c, coords[done], block], r2.at[2, hop - 1, c]
        else:
            here = lanes(c * 128, 128)
            source = acc.at[(m, *pick({done: coords[done], dim: block}), slice(None), here)]
            target = r2.at[m, hop - 1, :, :, here]
        return remote(source, target, s2.at[m, c, hop - 1], v2.at[m, c, hop - 1], ring[dim][hop - 1])

    def third_copy(m, hop):
        one, two, dim = ORDERS[m]
        block = (coords[dim] + hop) % 4
        source = acc.at[(m, *pick({one: coords[one], two: coords[two], dim: block}))]
        return remote(source, r3.at[m, hop - 1], s3.at[m, hop - 1], v3.at[m, hop - 1], ring[dim][hop - 1])

    def first_send(m, c):
        pair_add(m, c)
        for hop in HOPS:
            first_copy(m, c, hop).start()

    def second_send(m, c):
        dim = ORDERS[m][0]
        for hop in HOPS:
            first_copy(m, c, hop).wait_recv()
        if m == 2:
            total = acc[2, c, coords[dim]].astype(F32)
            for slot in range(3):
                total = total + r1[2, slot, c].astype(F32)
            acc[2, c, coords[dim]] = total.astype(BF16)
        else:
            here = lanes(c * 128, 128)
            where = (m, *pick({dim: coords[dim]}), slice(None), here)
            total = acc[where].astype(F32)
            for slot in range(3):
                total = total + r1[m, slot, :, :, :, here].astype(F32)
            acc[where] = total.astype(BF16)
        for hop in HOPS:
            second_copy(m, c, hop).start()

    def second_add(m, c):
        one, two = ORDERS[m][:2]
        for hop in HOPS:
            second_copy(m, c, hop).wait_recv()
        if m == 2:
            where = (2, c, coords[one], coords[two])
            total = acc[where].astype(F32)
            for slot in range(3):
                total = total + r2[2, slot, c].astype(F32)
        else:
            here = lanes(c * 128, 128)
            where = (m, *pick({one: coords[one], two: coords[two]}), slice(None), here)
            total = acc[where].astype(F32)
            for slot in range(3):
                total = total + r2[m, slot, :, :, here].astype(F32)
        acc[where] = total.astype(BF16)

    def third_send(m):
        for hop in HOPS:
            third_copy(m, hop).start()

    def last_send(m):
        for hop in HOPS:
            third_copy(m, hop).wait_recv()
        total = acc[(m, *coords)].astype(F32)
        for slot in range(3):
            total = total + r3[m, slot].astype(F32)
        fin[m, 0] = total[:8]
        fin[m, 1] = total[8:]
        last_copy(m).start()

    def last_copy(m):
        return remote(fin.at[m, 1 - core], fin_r.at[m], fin_s.at[m], fin_v.at[m], twin)

    def chunk(c, carry):
        edge_chunk(c)

        @pl.when(c > 0)
        def _():
            node_chunk(c - 1)
            first_send(0, c - 1)

        @pl.when(c > 1)
        def _():
            first_send(1, c - 2)
            first_send(2, c - 2)
            second_send(0, c - 2)

        @pl.when(c > 2)
        def _():
            second_send(1, c - 3)
            second_send(2, c - 3)
            second_add(0, c - 3)

        return carry

    lax.fori_loop(0, N_CHUNK, chunk, 0)

    def bias_send(stage):
        if stage == 3:
            return [go(remote(b_acc.at[3], b_r.at[9], b_s.at[9], b_v.at[9], twin))]
        started = []
        for hop in range(3):
            slot = 3 * stage + hop
            started.append(go(remote(
                b_acc.at[stage], b_r.at[slot], b_s.at[slot], b_v.at[slot],
                ring[BIAS_ORDER[stage]][hop],
            )))
        return started

    def bias_add(stage, copies):
        total = b_acc[stage]
        for copy in copies:
            copy.wait_recv()
        for slot in range(3 * stage, 3 * stage + len(copies)):
            total = total + b_r[slot]
        return total

    def token_grad_block(i):
        here = pl.ds(i * 256, 256)
        stage[here, :] = dot_cols(back[here, :], w_src[...]).astype(BF16)
        copy = pltpu.make_async_copy(stage.at[here], token_grad_hbm.at[here], out_sem.at[i])
        copy.start()
        return copy

    for i in range(8):
        b_acc[0, i : i + 1, :] = jnp.sum(bias_sum[:, i * 128 : i * 128 + 128], axis=0, keepdims=True)
    b_copies = bias_send(0)
    first_send(0, 3)
    first_send(1, 2)
    first_send(2, 2)
    second_send(0, 2)
    second_send(1, 1)
    second_send(2, 1)
    written = [token_grad_block(0)]
    node_chunk(3)
    b_acc[1] = bias_add(0, b_copies)
    b_copies = bias_send(1)
    written.append(token_grad_block(1))
    first_send(1, 3)
    first_send(2, 3)
    second_send(0, 3)
    second_send(1, 2)
    second_send(2, 2)
    b_acc[2] = bias_add(1, b_copies)
    b_copies = bias_send(2)
    second_add(0, 1)
    second_add(0, 2)
    second_add(1, 0)
    second_add(2, 0)
    written.append(token_grad_block(2))
    second_send(1, 3)
    second_send(2, 3)
    second_add(0, 3)
    third_send(0)
    b_acc[3] = bias_add(2, b_copies)
    b_copies = bias_send(3)
    second_add(1, 1)
    second_add(2, 1)
    second_add(1, 2)
    second_add(2, 2)
    written.append(token_grad_block(3))
    second_add(1, 3)
    third_send(1)
    second_add(2, 3)
    third_send(2)
    updated_ref[...] = (nodes[...].astype(F32) + dot(nsum[...], w_out[...])).astype(BF16)
    node_grad_ref[...] = (cot[...].astype(F32) + dot_cols(nback[...], w_dst[...])).astype(BF16)
    o_bias[...] = bias_add(3, b_copies)
    for m in range(3):
        last_send(m)
    for m in range(3):
        last_copy(m).wait_recv()
        if m == 2:
            outs[m][:, lanes(core * 512, 512)] = fin[m, core]
            outs[m][:, lanes((1 - core) * 512, 512)] = fin_r[m]
        else:
            for c in range(N_CHUNK):
                part_c = pl.ds(c * 128, 128)
                outs[m][:, lanes(c * CHUNK + core * 128, 128)] = fin[m, core, :, part_c]
                outs[m][:, lanes(c * CHUNK + (1 - core) * 128, 128)] = fin_r[m, :, part_c]
    for copy in written:
        copy.wait()
    for copy in sends:
        copy.wait_send()

    def settle(c, carry):
        for slot in (1, 2, 3, 4):
            near_copy(c, slot).wait_send()
            part_copy(c, slot).wait_send()
        for m in range(3):
            pair_copy(m, c).wait_send()
            for hop in HOPS:
                first_copy(m, c, hop).wait_send()
                second_copy(m, c, hop).wait_send()
        return carry

    lax.fori_loop(0, N_CHUNK, settle, 0)
    for m in range(3):
        last_copy(m).wait_send()
        for hop in HOPS:
            third_copy(m, hop).wait_send()


def finish_kernel(*refs):
    ins, b_ref, outs, o_ref, held, in_sems, out_sems = refs[:6], refs[6], refs[7:13], refs[13], refs[14:20], refs[20], refs[21]
    copies = []
    for i, (source, target) in enumerate(zip(ins, outs)):
        pieces = 4 if source.shape[0] == 1024 else 1
        size = source.shape[0] // pieces
        for piece in range(pieces):
            here = pl.ds(piece * size, size)
            copies.append((
                pltpu.make_async_copy(source.at[here], held[i].at[here], in_sems.at[i, piece]),
                pltpu.make_async_copy(held[i].at[here], target.at[here], out_sems.at[i, piece]),
            ))
    for fetch, _ in copies:
        fetch.start()
    index = lax.axis_index("region") * 8 + lax.axis_index("sub")
    turned = pltpu.roll(b_ref[...], (128 - index % 16 * 8) % 128, axis=1)
    own = lax.broadcasted_iota(jnp.int32, (8, 128), 0) == index // 16
    o_ref[...] = jnp.sum(jnp.where(own, turned, 0.0), axis=0, keepdims=True)[:, :8]
    for fetch, store in copies:
        fetch.wait()
        store.start()
    for _, store in copies:
        store.wait()


def finish(arrays, bias_sums):
    vmem = pl.BlockSpec(memory_space=pltpu.VMEM)
    hbm = pl.BlockSpec(memory_space=pl.ANY)
    *results, part_bias = pl.pallas_call(
        finish_kernel,
        out_shape=(
            *[jax.ShapeDtypeStruct(a.shape, a.dtype) for a in arrays],
            jax.ShapeDtypeStruct((1, 8), F32),
        ),
        in_specs=[hbm] * 6 + [vmem],
        out_specs=[hbm] * 6 + [vmem],
        scratch_shapes=[
            *[pltpu.VMEM(a.shape, a.dtype) for a in arrays],
            pltpu.SemaphoreType.DMA((6, 4)), pltpu.SemaphoreType.DMA((6, 4)),
        ],
        compiler_params=pltpu.CompilerParams(vmem_limit_bytes=60 * 1024 * 1024),
        name="finish",
    )(*arrays, bias_sums)
    return (*results, part_bias.reshape(8))


def body(tokens, nodes, dests, token_count, w_src, w_dst, bias, w_out, cotangent):
    dma = pltpu.SemaphoreType.DMA
    vmem = pl.BlockSpec(memory_space=pltpu.VMEM)
    hbm = pl.BlockSpec(memory_space=pl.ANY)
    slab = jax.ShapeDtypeStruct((8, 1024), F32)
    node_like = jax.ShapeDtypeStruct((NODE, 1024), BF16)
    whole = (1024, 1024)
    updated, token_grad, node_grad, o_src, o_dst, o_out, o_bias = pl.pallas_call(
        layer_kernel,
        out_shape=(
            node_like, jax.ShapeDtypeStruct(whole, BF16), node_like, slab, slab, slab,
            jax.ShapeDtypeStruct((8, 128), F32),
        ),
        in_specs=[hbm, hbm, vmem, vmem, hbm, hbm, vmem, hbm, hbm],
        out_specs=[vmem, hbm, vmem, vmem, vmem, vmem, vmem],
        scratch_shapes=[
            pltpu.VMEM(whole, BF16), pltpu.VMEM((NODE, 1024), BF16), pltpu.VMEM(whole, BF16),
            pltpu.VMEM(whole, BF16), pltpu.VMEM(whole, BF16), pltpu.VMEM((NODE, 1024), BF16),
            pltpu.VMEM(whole, BF16), pltpu.VMEM((1024, NODE), BF16), pltpu.VMEM((8, 1024), jnp.int32),
            pltpu.VMEM((2048, PAD), BF16), pltpu.VMEM((NEAR, 2048), BF16),
            pltpu.VMEM((N_CHUNK, PAD, 2 * CHUNK), BF16), pltpu.VMEM((2048, 2 * CHUNK), BF16),
            pltpu.VMEM(whole, BF16), pltpu.VMEM((N_CHUNK, NEAR, 2 * CHUNK), BF16),
            pltpu.VMEM((N_CHUNK, 4, NODE, 2 * CHUNK), BF16), pltpu.VMEM((NODE, 1024), BF16),
            pltpu.VMEM((NODE, 1024), BF16), pltpu.VMEM((3, 4, 4, 4, 16, 1024), BF16),
            pltpu.VMEM(whole, BF16), pltpu.VMEM((8, 1024), F32),
            pltpu.VMEM((3, 4, 4, 4, 16, 512), BF16),
            pltpu.VMEM((3, 4, 4, 4, 16, 512), BF16),
            pltpu.VMEM((3, 3, 4, 4, 16, 512), BF16),
            pltpu.VMEM((3, 3, 4, 16, 512), BF16),
            pltpu.VMEM((3, 3, 16, 512), BF16),
            pltpu.VMEM((3, 2, 8, 512), F32),
            pltpu.VMEM((3, 8, 512), F32),
            pltpu.VMEM((4, 8, 128), F32),
            pltpu.VMEM((10, 8, 128), F32),
            dma((6,)), dma((4,)), dma((4, 4)), dma((4, 4)), dma((4, 4)), dma((4, 4)),
            dma((3, 4)), dma((3, 4)), dma((3, 4, 3)), dma((3, 4, 3)), dma((3, 4, 3)), dma((3, 4, 3)),
            dma((3, 3)), dma((3, 3)), dma((3,)), dma((3,)), dma((10,)), dma((10,)),
        ],
        compiler_params=pltpu.CompilerParams(
            collective_id=1, has_side_effects=True, vmem_limit_bytes=60 * 1024 * 1024
        ),
        name="layer",
    )(
        tokens, nodes, dests.T, token_count.reshape(1, 1), w_src, w_dst, bias.reshape(1, 1024), w_out, cotangent,
    )
    return finish((updated, token_grad, node_grad, o_src, o_dst, o_out), o_bias)


def solution(mesh):
    return jax.shard_map(
        body,
        mesh=mesh,
        in_specs=(
            P(("region", "sub"), None),
            P(("region", "sub"), None),
            P(("region", "sub"), None),
            P(("region", "sub")),
            P(),
            P(),
            P(),
            P(),
            P(("region", "sub"), None),
        ),
        out_specs=(
            P(("region", "sub"), None),
            P(("region", "sub"), None),
            P(("region", "sub"), None),
            P(("region", "sub"), None),
            P(("region", "sub"), None),
            P(("region", "sub"), None),
            P(("region", "sub")),
        ),
        check_vma=False,
    )
```

```python
import jax
import jax.numpy as jnp
from jax import lax
from jax.experimental import pallas as pl
from jax.experimental.pallas import tpu as pltpu
from jax.sharding import PartitionSpec as P

MESH = pl.DeviceIdType.MESH
F32, BF16 = jnp.float32, jnp.bfloat16
NODE = 160
NEAR = 5 * NODE
PAD = 896
CHUNK = 256
N_CHUNK = 4
DIMS = (0, 1, 2)
ORDERS = ((2, 0, 1), (0, 1, 2), (1, 2, 0))
BIAS_ORDER = (2, 1, 0)
HOPS = (2, 1, 3)


def device_at(coords, core):
    return (coords[0] * 4 + coords[1], coords[2] * 2 + core)


def moved(coords, dim, value):
    return tuple(value if d == dim else c for d, c in enumerate(coords))


def pick(blocks):
    return tuple(blocks.get(d, slice(None)) for d in DIMS)


def dot(left, right):
    return jnp.dot(left, right, preferred_element_type=F32)


def dot_cols(left, right):
    return lax.dot_general(left, right, (((1,), (1,)), ((), ())), preferred_element_type=F32)


def dot_rows(left, right):
    return lax.dot_general(left, right, (((0,), (0,)), ((), ())), preferred_element_type=F32)


def lanes(start, size):
    return pl.ds(pl.multiple_of(start, 128), size)


def rows(start, size):
    return pl.ds(pl.multiple_of(start, 16), size)


def layer_kernel(
    tokens_hbm, nodes_hbm, dests_ref, count_ref, w_src_hbm, w_dst_hbm, bias_ref, w_out_hbm, cot_hbm,
    updated_ref, token_grad_hbm, node_grad_ref, o_src, o_dst, o_out, o_bias,
    tokens, nodes, w_src, w_dst, w_out, cot, tokens_t, nodes_t, ids, onehot, onehot_t, near, edges,
    back, part, rpart, nsum, nback, grads, stage, bias_sum,
    acc, pair, r1, r2, r3, fin, fin_r, b_acc, b_r,
    in_sem, out_sem, near_s, near_v, part_s, part_v,
    pair_s, pair_v, s1, v1, s2, v2, s3, v3, fin_s, fin_v, b_s, b_v,
):
    region, sub = lax.axis_index("region"), lax.axis_index("sub")
    n_region, n_sub = 16, 8
    coords, core = (region // 4, region % 4, sub // 2), sub % 2
    twin = device_at(coords, 1 - core)
    ring = [
        [device_at(moved(coords, dim, (coords[dim] + hop) % 4), core) for hop in (1, 2, 3)]
        for dim in DIMS
    ]
    around = [
        (region, sub),
        ((region + n_region - 1) % n_region, sub),
        ((region + 1) % n_region, sub),
        (region, (sub + n_sub - 1) % n_sub),
        (region, (sub + 1) % n_sub),
    ]
    facing = (0, 2, 1, 4, 3)
    outs = (o_src, o_dst, o_out)
    sends = []

    def remote(source, target, send, recv, device):
        return pltpu.make_async_remote_copy(
            src_ref=source, dst_ref=target, send_sem=send, recv_sem=recv,
            device_id=device, device_id_type=MESH,
        )

    def go(copy):
        copy.start()
        sends.append(copy)
        return copy

    loads = [
        pltpu.make_async_copy(source, target, in_sem.at[i])
        for i, (source, target) in enumerate((
            (nodes_hbm, nodes), (cot_hbm, cot), (w_dst_hbm, w_dst), (w_out_hbm, w_out),
            (w_src_hbm, w_src), (tokens_hbm, tokens),
        ))
    ]
    for load in loads[:4]:
        load.start()
    barrier = pltpu.get_barrier_semaphore()
    peers = [twin] + ring[0] + ring[1] + ring[2] + around[1:]
    for peer in peers:
        pl.semaphore_signal(barrier, inc=1, device_id=peer, device_id_type=MESH)

    def near_copy(c, slot):
        return remote(
            near.at[c, pl.ds(0, NODE)], near.at[c, pl.ds(slot * NODE, NODE)],
            near_s.at[c, slot - 1], near_v.at[c, slot - 1], around[facing[slot]],
        )

    def part_copy(c, slot):
        return remote(
            part.at[c, pl.ds(slot * NODE, NODE)], rpart.at[c, facing[slot] - 1],
            part_s.at[c, facing[slot] - 1], part_v.at[c, facing[slot] - 1], around[slot],
        )

    def pair_copy(m, c):
        if m == 2:
            return remote(
                grads.at[2, c, :, :, :, lanes((1 - core) * 512, 512)], pair.at[2, c],
                pair_s.at[2, c], pair_v.at[2, c], twin,
            )
        return remote(
            grads.at[m, :, :, :, :, lanes(c * CHUNK + (1 - core) * 128, 128)],
            pair.at[m, :, :, :, :, lanes(c * 128, 128)],
            pair_s.at[m, c], pair_v.at[m, c], twin,
        )

    def project(c):
        span = pl.ds(pl.multiple_of(c * CHUNK, CHUNK), CHUNK)
        near[c, :NODE, :CHUNK] = dot(nodes[...], w_dst[:, span]).astype(BF16)
        near[c, :NODE, CHUNK:] = dot_cols(cot[...], w_out[span, :]).astype(BF16)
        near[c, NEAR:, :] = jnp.zeros((PAD - NEAR, 2 * CHUNK), BF16)

    def send_near(c):
        for slot in (1, 2, 3, 4):
            near_copy(c, slot).start()

    def project_later(c, carry):
        project(c)
        return carry

    for load in loads[:4]:
        load.wait()
    for load in loads[4:]:
        load.start()
    project(0)
    pl.semaphore_wait(barrier, len(peers))
    send_near(0)

    live = lax.broadcasted_iota(jnp.int32, (2, 1024), 1) < count_ref[...]
    ids[...] = jnp.zeros((8, 1024), jnp.int32)
    ids[:2] = jnp.where(live, dests_ref[...], -1)
    ids_t = ids[...].T
    base = [(around[s][0] * n_sub + around[s][1]) * NODE for s in range(5)]

    def node_ids(shape, dim):
        place = lax.broadcasted_iota(jnp.int32, shape, dim)
        value = jnp.full(shape, -2, jnp.int32)
        for s in range(4, -1, -1):
            value = jnp.where(place < (s + 1) * NODE, place + (base[s] - s * NODE), value)
        return value

    across, down = node_ids((1, PAD), 1), node_ids((NEAR, 1), 0)
    for tb in range(4):
        for k in range(2):
            here = (tb // 2 * 2 + k) * 512 + tb % 2 * 256
            onehot[here : here + 256, :] = jnp.where(
                ids_t[tb * 256 : tb * 256 + 256, k : k + 1] == across, 1.0, 0.0
            ).astype(BF16)
            onehot_t[:, here : here + 256] = jnp.where(
                down == ids[k : k + 1, tb * 256 : tb * 256 + 256], 1.0, 0.0
            ).astype(BF16)

    lax.fori_loop(1, N_CHUNK, project_later, 0)
    send_near(1)
    nodes_t[...] = nodes[...].T
    for load in loads[4:]:
        load.wait()

    def turn(i, carry):
        tokens_t[:, lanes(i * 256, 256)] = tokens[rows(i * 256, 256), :].T
        return carry

    lax.fori_loop(0, 4, turn, 0)
    bias_sum[...] = jnp.zeros((8, 1024), F32)

    def edge_chunk(c):
        span = pl.ds(pl.multiple_of(c * CHUNK, CHUNK), CHUNK)
        for slot in (1, 2, 3, 4):
            near_copy(c, slot).wait_recv()

        @pl.when(c < N_CHUNK - 2)
        def _():
            send_near(c + 2)

        def token_block(tb, carry):
            here = rows(tb * 512, 512)
            plain = dot(tokens[here, :], w_src[:, span]) + bias_ref[:, span]
            total = jnp.zeros((512, CHUNK), F32)
            both = dot(onehot[rows(tb * 1024, 1024), :], near[c])
            for k in range(2):
                there = rows((tb * 2 + k) * 512, 512)
                found = both[k * 512 : k * 512 + 512]
                preact = plain + found[:, :CHUNK]
                sigma = 0.5 * jnp.tanh(0.5 * preact) + 0.5
                act = preact * sigma
                grad = found[:, CHUNK:] * (sigma + act * (1.0 - sigma))
                edges[there, :CHUNK] = act.astype(BF16)
                edges[there, CHUNK:] = grad.astype(BF16)
                total = total + grad
            back[here, span] = total.astype(BF16)
            bias_sum[:, span] += jnp.sum(total.reshape(64, 8, CHUNK), axis=0)
            return carry

        lax.fori_loop(0, 2, token_block, 0, unroll=2)

        part[c] = dot(onehot_t[...], edges[...]).astype(BF16)
        for slot in (1, 2, 3, 4):
            part_copy(c, slot).start()

    def source_chunk(c):
        span = pl.ds(pl.multiple_of(c * CHUNK, CHUNK), CHUNK)
        value = dot(tokens_t[...], back[:, span])
        grads[0, :, :, :, :, span] = value.astype(BF16).reshape(4, 4, 4, 16, CHUNK)
        pair_copy(0, c).start()

    def node_chunk(c):
        span = pl.ds(pl.multiple_of(c * CHUNK, CHUNK), CHUNK)
        total = part[c, :NODE].astype(F32)
        for slot in (1, 2, 3, 4):
            part_copy(c, facing[slot]).wait_recv()
            total = total + rpart[c, slot - 1].astype(F32)
        total = total.astype(BF16)
        nsum[:, span] = total[:, :CHUNK]
        nback[:, span] = total[:, CHUNK:]

        value = dot(nodes_t[...], nback[:, span])
        grads[1, :, :, :, :, span] = value.astype(BF16).reshape(4, 4, 4, 16, CHUNK)
        pair_copy(1, c).start()
        value = dot_rows(nsum[:, span], cot[...])
        grads[2, c] = value.astype(BF16).reshape(4, 4, 16, 1024)
        pair_copy(2, c).start()

    def pair_add(m, c):
        pair_copy(m, c).wait_recv()
        if m == 2:
            acc[2, c] = grads[2, c, :, :, :, lanes(core * 512, 512)] + pair[2, c]
            return
        here = lanes(c * 128, 128)
        own = grads[m, :, :, :, :, lanes(c * CHUNK + core * 128, 128)]
        acc[m, :, :, :, :, here] = own + pair[m, :, :, :, :, here]

    def first_copy(m, c, hop):
        dim = ORDERS[m][0]
        block = (coords[dim] + hop) % 4
        if m == 2:
            source, target = acc.at[2, c, block], r1.at[2, hop - 1, c]
        else:
            here = lanes(c * 128, 128)
            source = acc.at[(m, *pick({dim: block}), slice(None), here)]
            target = r1.at[m, hop - 1, :, :, :, here]
        return remote(source, target, s1.at[m, c, hop - 1], v1.at[m, c, hop - 1], ring[dim][hop - 1])

    def second_copy(m, c, hop):
        done, dim = ORDERS[m][:2]
        block = (coords[dim] + hop) % 4
        if m == 2:
            source, target = acc.at[2, c, coords[done], block], r2.at[2, hop - 1, c]
        else:
            here = lanes(c * 128, 128)
            source = acc.at[(m, *pick({done: coords[done], dim: block}), slice(None), here)]
            target = r2.at[m, hop - 1, :, :, here]
        return remote(source, target, s2.at[m, c, hop - 1], v2.at[m, c, hop - 1], ring[dim][hop - 1])

    def third_copy(m, hop):
        one, two, dim = ORDERS[m]
        block = (coords[dim] + hop) % 4
        source = acc.at[(m, *pick({one: coords[one], two: coords[two], dim: block}))]
        return remote(source, r3.at[m, hop - 1], s3.at[m, hop - 1], v3.at[m, hop - 1], ring[dim][hop - 1])

    def first_send(m, c):
        pair_add(m, c)
        for hop in HOPS:
            first_copy(m, c, hop).start()

    def second_send(m, c):
        dim = ORDERS[m][0]
        for hop in HOPS:
            first_copy(m, c, hop).wait_recv()
        if m == 2:
            total = acc[2, c, coords[dim]].astype(F32)
            for slot in range(3):
                total = total + r1[2, slot, c].astype(F32)
            acc[2, c, coords[dim]] = total.astype(BF16)
        else:
            here = lanes(c * 128, 128)
            where = (m, *pick({dim: coords[dim]}), slice(None), here)
            total = acc[where].astype(F32)
            for slot in range(3):
                total = total + r1[m, slot, :, :, :, here].astype(F32)
            acc[where] = total.astype(BF16)
        for hop in HOPS:
            second_copy(m, c, hop).start()

    def second_add(m, c):
        one, two = ORDERS[m][:2]
        for hop in HOPS:
            second_copy(m, c, hop).wait_recv()
        if m == 2:
            where = (2, c, coords[one], coords[two])
            total = acc[where].astype(F32)
            for slot in range(3):
                total = total + r2[2, slot, c].astype(F32)
        else:
            here = lanes(c * 128, 128)
            where = (m, *pick({one: coords[one], two: coords[two]}), slice(None), here)
            total = acc[where].astype(F32)
            for slot in range(3):
                total = total + r2[m, slot, :, :, here].astype(F32)
        acc[where] = total.astype(BF16)

    def third_send(m):
        for hop in HOPS:
            third_copy(m, hop).start()

    def last_send(m):
        for hop in HOPS:
            third_copy(m, hop).wait_recv()
        total = acc[(m, *coords)].astype(F32)
        for slot in range(3):
            total = total + r3[m, slot].astype(F32)
        fin[m, 0] = total[:8]
        fin[m, 1] = total[8:]
        last_copy(m).start()

    def last_copy(m):
        return remote(fin.at[m, 1 - core], fin_r.at[m], fin_s.at[m], fin_v.at[m], twin)

    def chunk(c, carry):
        @pl.when(c == N_CHUNK - 1)
        def _():
            first_send(0, 1)
            first_send(1, 0)
            first_send(2, 0)

        edge_chunk(c)

        @pl.when((c > 0) & (c < N_CHUNK - 1))
        def _():
            source_chunk(c - 1)

        @pl.when(c == N_CHUNK - 2)
        def _():
            node_chunk(0)
            first_send(0, 0)

        return carry

    lax.fori_loop(0, N_CHUNK, chunk, 0)

    def bias_send(stage):
        if stage == 3:
            return [go(remote(b_acc.at[3], b_r.at[9], b_s.at[9], b_v.at[9], twin))]
        started = []
        for hop in range(3):
            slot = 3 * stage + hop
            started.append(go(remote(
                b_acc.at[stage], b_r.at[slot], b_s.at[slot], b_v.at[slot],
                ring[BIAS_ORDER[stage]][hop],
            )))
        return started

    def bias_add(stage, copies):
        total = b_acc[stage]
        for copy in copies:
            copy.wait_recv()
        for slot in range(3 * stage, 3 * stage + len(copies)):
            total = total + b_r[slot]
        return total

    def token_grad_block(i):
        here = pl.ds(i * 256, 256)
        stage[here, :] = dot_cols(back[here, :], w_src[...]).astype(BF16)
        copy = pltpu.make_async_copy(stage.at[here], token_grad_hbm.at[here], out_sem.at[i])
        copy.start()
        return copy

    for i in range(8):
        b_acc[0, i : i + 1, :] = jnp.sum(bias_sum[:, i * 128 : i * 128 + 128], axis=0, keepdims=True)
    b_copies = bias_send(0)
    source_chunk(2)
    node_chunk(1)
    source_chunk(3)
    first_send(0, 2)
    second_send(0, 0)
    first_send(1, 1)
    first_send(2, 1)
    node_chunk(2)
    first_send(0, 3)
    second_send(0, 1)
    b_acc[1] = bias_add(0, b_copies)
    b_copies = bias_send(1)
    written = [token_grad_block(0)]
    first_send(1, 2)
    first_send(2, 2)
    second_send(1, 0)
    second_send(2, 0)
    node_chunk(3)
    second_send(1, 1)
    second_send(2, 1)
    first_send(1, 3)
    first_send(2, 3)
    second_send(0, 2)
    second_send(0, 3)
    second_send(1, 2)
    second_send(2, 2)
    b_acc[2] = bias_add(1, b_copies)
    b_copies = bias_send(2)
    written.append(token_grad_block(1))
    for m in range(3):
        second_add(m, 0)
        second_add(m, 1)
    second_send(1, 3)
    second_send(2, 3)
    for c in (2, 3):
        second_add(0, c)
    third_send(0)
    b_acc[3] = bias_add(2, b_copies)
    b_copies = bias_send(3)
    written.append(token_grad_block(2))
    second_add(1, 2)
    second_add(2, 2)
    second_add(1, 3)
    third_send(1)
    second_add(2, 3)
    third_send(2)
    written.append(token_grad_block(3))
    updated_ref[...] = (nodes[...].astype(F32) + dot(nsum[...], w_out[...])).astype(BF16)
    node_grad_ref[...] = (cot[...].astype(F32) + dot_cols(nback[...], w_dst[...])).astype(BF16)
    o_bias[...] = bias_add(3, b_copies)
    for m in range(3):
        last_send(m)
    for m in range(3):
        last_copy(m).wait_recv()
        if m == 2:
            outs[m][:, lanes(core * 512, 512)] = fin[m, core]
            outs[m][:, lanes((1 - core) * 512, 512)] = fin_r[m]
        else:
            for c in range(N_CHUNK):
                part_c = pl.ds(c * 128, 128)
                outs[m][:, lanes(c * CHUNK + core * 128, 128)] = fin[m, core, :, part_c]
                outs[m][:, lanes(c * CHUNK + (1 - core) * 128, 128)] = fin_r[m, :, part_c]
    for copy in written:
        copy.wait()
    for copy in sends:
        copy.wait_send()

    def settle(c, carry):
        for slot in (1, 2, 3, 4):
            near_copy(c, slot).wait_send()
            part_copy(c, slot).wait_send()
        for m in range(3):
            pair_copy(m, c).wait_send()
            for hop in HOPS:
                first_copy(m, c, hop).wait_send()
                second_copy(m, c, hop).wait_send()
        return carry

    lax.fori_loop(0, N_CHUNK, settle, 0)
    for m in range(3):
        last_copy(m).wait_send()
        for hop in HOPS:
            third_copy(m, hop).wait_send()


def finish_kernel(*refs):
    ins, b_ref, outs, o_ref, held, in_sems, out_sems = refs[:6], refs[6], refs[7:13], refs[13], refs[14:20], refs[20], refs[21]
    copies = []
    for i, (source, target) in enumerate(zip(ins, outs)):
        pieces = 4 if source.shape[0] == 1024 else 1
        size = source.shape[0] // pieces
        for piece in range(pieces):
            here = pl.ds(piece * size, size)
            copies.append((
                pltpu.make_async_copy(source.at[here], held[i].at[here], in_sems.at[i, piece]),
                pltpu.make_async_copy(held[i].at[here], target.at[here], out_sems.at[i, piece]),
            ))
    for fetch, _ in copies:
        fetch.start()
    index = lax.axis_index("region") * 8 + lax.axis_index("sub")
    turned = pltpu.roll(b_ref[...], (128 - index % 16 * 8) % 128, axis=1)
    own = lax.broadcasted_iota(jnp.int32, (8, 128), 0) == index // 16
    o_ref[...] = jnp.sum(jnp.where(own, turned, 0.0), axis=0, keepdims=True)[:, :8]
    for fetch, store in copies:
        fetch.wait()
        store.start()
    for _, store in copies:
        store.wait()


def finish(arrays, bias_sums):
    vmem = pl.BlockSpec(memory_space=pltpu.VMEM)
    hbm = pl.BlockSpec(memory_space=pl.ANY)
    *results, part_bias = pl.pallas_call(
        finish_kernel,
        out_shape=(
            *[jax.ShapeDtypeStruct(a.shape, a.dtype) for a in arrays],
            jax.ShapeDtypeStruct((1, 8), F32),
        ),
        in_specs=[hbm] * 6 + [vmem],
        out_specs=[hbm] * 6 + [vmem],
        scratch_shapes=[
            *[pltpu.VMEM(a.shape, a.dtype) for a in arrays],
            pltpu.SemaphoreType.DMA((6, 4)), pltpu.SemaphoreType.DMA((6, 4)),
        ],
        compiler_params=pltpu.CompilerParams(vmem_limit_bytes=60 * 1024 * 1024),
        name="finish",
    )(*arrays, bias_sums)
    return (*results, part_bias.reshape(8))


def body(tokens, nodes, dests, token_count, w_src, w_dst, bias, w_out, cotangent):
    dma = pltpu.SemaphoreType.DMA
    vmem = pl.BlockSpec(memory_space=pltpu.VMEM)
    hbm = pl.BlockSpec(memory_space=pl.ANY)
    slab = jax.ShapeDtypeStruct((8, 1024), F32)
    node_like = jax.ShapeDtypeStruct((NODE, 1024), BF16)
    whole = (1024, 1024)
    updated, token_grad, node_grad, o_src, o_dst, o_out, o_bias = pl.pallas_call(
        layer_kernel,
        out_shape=(
            node_like, jax.ShapeDtypeStruct(whole, BF16), node_like, slab, slab, slab,
            jax.ShapeDtypeStruct((8, 128), F32),
        ),
        in_specs=[hbm, hbm, vmem, vmem, hbm, hbm, vmem, hbm, hbm],
        out_specs=[vmem, hbm, vmem, vmem, vmem, vmem, vmem],
        scratch_shapes=[
            pltpu.VMEM(whole, BF16), pltpu.VMEM((NODE, 1024), BF16), pltpu.VMEM(whole, BF16),
            pltpu.VMEM(whole, BF16), pltpu.VMEM(whole, BF16), pltpu.VMEM((NODE, 1024), BF16),
            pltpu.VMEM(whole, BF16), pltpu.VMEM((1024, NODE), BF16), pltpu.VMEM((8, 1024), jnp.int32),
            pltpu.VMEM((2048, PAD), BF16), pltpu.VMEM((NEAR, 2048), BF16),
            pltpu.VMEM((N_CHUNK, PAD, 2 * CHUNK), BF16), pltpu.VMEM((2048, 2 * CHUNK), BF16),
            pltpu.VMEM(whole, BF16), pltpu.VMEM((N_CHUNK, NEAR, 2 * CHUNK), BF16),
            pltpu.VMEM((N_CHUNK, 4, NODE, 2 * CHUNK), BF16), pltpu.VMEM((NODE, 1024), BF16),
            pltpu.VMEM((NODE, 1024), BF16), pltpu.VMEM((3, 4, 4, 4, 16, 1024), BF16),
            pltpu.VMEM(whole, BF16), pltpu.VMEM((8, 1024), F32),
            pltpu.VMEM((3, 4, 4, 4, 16, 512), BF16),
            pltpu.VMEM((3, 4, 4, 4, 16, 512), BF16),
            pltpu.VMEM((3, 3, 4, 4, 16, 512), BF16),
            pltpu.VMEM((3, 3, 4, 16, 512), BF16),
            pltpu.VMEM((3, 3, 16, 512), BF16),
            pltpu.VMEM((3, 2, 8, 512), F32),
            pltpu.VMEM((3, 8, 512), F32),
            pltpu.VMEM((4, 8, 128), F32),
            pltpu.VMEM((10, 8, 128), F32),
            dma((6,)), dma((4,)), dma((4, 4)), dma((4, 4)), dma((4, 4)), dma((4, 4)),
            dma((3, 4)), dma((3, 4)), dma((3, 4, 3)), dma((3, 4, 3)), dma((3, 4, 3)), dma((3, 4, 3)),
            dma((3, 3)), dma((3, 3)), dma((3,)), dma((3,)), dma((10,)), dma((10,)),
        ],
        compiler_params=pltpu.CompilerParams(
            collective_id=1, has_side_effects=True, vmem_limit_bytes=60 * 1024 * 1024
        ),
        name="layer",
    )(
        tokens, nodes, dests.T, token_count.reshape(1, 1), w_src, w_dst, bias.reshape(1, 1024), w_out, cotangent,
    )
    return finish((updated, token_grad, node_grad, o_src, o_dst, o_out), o_bias)


def solution(mesh):
    return jax.shard_map(
        body,
        mesh=mesh,
        in_specs=(
            P(("region", "sub"), None),
            P(("region", "sub"), None),
            P(("region", "sub"), None),
            P(("region", "sub")),
            P(),
            P(),
            P(),
            P(),
            P(("region", "sub"), None),
        ),
        out_specs=(
            P(("region", "sub"), None),
            P(("region", "sub"), None),
            P(("region", "sub"), None),
            P(("region", "sub"), None),
            P(("region", "sub"), None),
            P(("region", "sub"), None),
            P(("region", "sub")),
        ),
        check_vma=False,
    )
```

```python
import jax
import jax.numpy as jnp
from jax import lax
from jax.experimental import pallas as pl
from jax.experimental.pallas import tpu as pltpu
from jax.sharding import PartitionSpec as P

MESH = pl.DeviceIdType.MESH
F32, BF16 = jnp.float32, jnp.bfloat16
NODE = 160
NEAR = 5 * NODE
PAD = 896
CHUNK = 256
N_CHUNK = 4
DIMS = (0, 1, 2)
ORDERS = ((2, 0, 1), (0, 1, 2), (1, 2, 0))
BIAS_ORDER = (2, 1, 0)
HOPS = (2, 1, 3)
LAST = ((2, True), (2, False), (1, True), (3, True), (1, False), (3, False), (0, True))


def device_at(coords, core):
    return (coords[0] * 4 + coords[1], coords[2] * 2 + core)


def moved(coords, dim, value):
    return tuple(value if d == dim else c for d, c in enumerate(coords))


def pick(blocks):
    return tuple(blocks.get(d, slice(None)) for d in DIMS)


def dot(left, right):
    return jnp.dot(left, right, preferred_element_type=F32)


def dot_cols(left, right):
    return lax.dot_general(left, right, (((1,), (1,)), ((), ())), preferred_element_type=F32)


def dot_rows(left, right):
    return lax.dot_general(left, right, (((0,), (0,)), ((), ())), preferred_element_type=F32)


def lanes(start, size):
    return pl.ds(pl.multiple_of(start, 128), size)


def rows(start, size):
    return pl.ds(pl.multiple_of(start, 16), size)


def layer_kernel(
    tokens_hbm, nodes_hbm, dests_ref, count_ref, w_src_hbm, w_dst_hbm, bias_ref, w_out_hbm, cot_hbm,
    updated_ref, token_grad_hbm, node_grad_ref, o_src, o_dst, o_out, o_bias,
    tokens, nodes, w_src, w_dst, w_out, cot, tokens_t, nodes_t, ids, onehot, onehot_t, near, edges,
    back, part, rpart, nsum, nback, grads, stage, bias_sum,
    acc, pair, r1, r2, r3, fin, b_acc, b_r,
    in_sem, out_sem, near_s, near_v, part_s, part_v,
    pair_s, pair_v, s1, v1, s2, v2, s3, v3, b_s, b_v,
):
    region, sub = lax.axis_index("region"), lax.axis_index("sub")
    n_region, n_sub = 16, 8
    coords, core = (region // 4, region % 4, sub // 2), sub % 2
    twin = device_at(coords, 1 - core)
    ring = [
        [device_at(moved(coords, dim, (coords[dim] + hop) % 4), core) for hop in (1, 2, 3)]
        for dim in DIMS
    ]
    around = [
        (region, sub),
        ((region + n_region - 1) % n_region, sub),
        ((region + 1) % n_region, sub),
        (region, (sub + n_sub - 1) % n_sub),
        (region, (sub + 1) % n_sub),
    ]
    facing = (0, 2, 1, 4, 3)
    outs = (o_src, o_dst, o_out)
    ring_twin = [
        [device_at(moved(coords, dim, (coords[dim] + hop) % 4), 1 - core) for hop in range(4)]
        for dim in DIMS
    ]
    sends = []

    def remote(source, target, send, recv, device):
        return pltpu.make_async_remote_copy(
            src_ref=source, dst_ref=target, send_sem=send, recv_sem=recv,
            device_id=device, device_id_type=MESH,
        )

    def go(copy):
        copy.start()
        sends.append(copy)
        return copy

    loads = [
        pltpu.make_async_copy(source, target, in_sem.at[i])
        for i, (source, target) in enumerate((
            (nodes_hbm, nodes), (cot_hbm, cot), (w_dst_hbm, w_dst), (w_out_hbm, w_out),
            (w_src_hbm, w_src), (tokens_hbm, tokens),
        ))
    ]
    for load in loads[:4]:
        load.start()
    barrier = pltpu.get_barrier_semaphore()
    peers = [twin] + ring[0] + ring[1] + ring[2] + around[1:]
    peers += ring_twin[0][1:] + ring_twin[1][1:] + ring_twin[2][1:]
    for peer in peers:
        pl.semaphore_signal(barrier, inc=1, device_id=peer, device_id_type=MESH)

    def near_copy(c, slot):
        return remote(
            near.at[c, pl.ds(0, NODE)], near.at[c, pl.ds(slot * NODE, NODE)],
            near_s.at[c, slot - 1], near_v.at[c, slot - 1], around[facing[slot]],
        )

    def part_copy(c, slot):
        return remote(
            part.at[c, pl.ds(slot * NODE, NODE)], rpart.at[c, facing[slot] - 1],
            part_s.at[c, facing[slot] - 1], part_v.at[c, facing[slot] - 1], around[slot],
        )

    def pair_copy(m, c):
        if m == 2:
            return remote(
                grads.at[2, c, :, :, :, lanes((1 - core) * 512, 512)], pair.at[2, c],
                pair_s.at[2, c], pair_v.at[2, c], twin,
            )
        return remote(
            grads.at[m, :, :, :, :, lanes(c * CHUNK + (1 - core) * 128, 128)],
            pair.at[m, :, :, :, :, lanes(c * 128, 128)],
            pair_s.at[m, c], pair_v.at[m, c], twin,
        )

    def project(c):
        span = pl.ds(pl.multiple_of(c * CHUNK, CHUNK), CHUNK)
        near[c, :NODE, :CHUNK] = dot(nodes[...], w_dst[:, span]).astype(BF16)
        near[c, :NODE, CHUNK:] = dot_cols(cot[...], w_out[span, :]).astype(BF16)
        near[c, NEAR:, :] = jnp.zeros((PAD - NEAR, 2 * CHUNK), BF16)

    def send_near(c):
        for slot in (1, 2, 3, 4):
            near_copy(c, slot).start()

    def project_later(c, carry):
        project(c)
        return carry

    for load in loads[:4]:
        load.wait()
    for load in loads[4:]:
        load.start()
    project(0)
    pl.semaphore_wait(barrier, len(peers))
    send_near(0)

    live = lax.broadcasted_iota(jnp.int32, (2, 1024), 1) < count_ref[...]
    ids[...] = jnp.zeros((8, 1024), jnp.int32)
    ids[:2] = jnp.where(live, dests_ref[...], -1)
    ids_t = ids[...].T
    base = [(around[s][0] * n_sub + around[s][1]) * NODE for s in range(5)]

    def node_ids(shape, dim):
        place = lax.broadcasted_iota(jnp.int32, shape, dim)
        value = jnp.full(shape, -2, jnp.int32)
        for s in range(4, -1, -1):
            value = jnp.where(place < (s + 1) * NODE, place + (base[s] - s * NODE), value)
        return value

    across, down = node_ids((1, PAD), 1), node_ids((NEAR, 1), 0)
    for tb in range(4):
        for k in range(2):
            here = (tb // 2 * 2 + k) * 512 + tb % 2 * 256
            onehot[here : here + 256, :] = jnp.where(
                ids_t[tb * 256 : tb * 256 + 256, k : k + 1] == across, 1.0, 0.0
            ).astype(BF16)
            onehot_t[:, here : here + 256] = jnp.where(
                down == ids[k : k + 1, tb * 256 : tb * 256 + 256], 1.0, 0.0
            ).astype(BF16)

    lax.fori_loop(1, N_CHUNK, project_later, 0)
    send_near(1)
    nodes_t[...] = nodes[...].T
    for load in loads[4:]:
        load.wait()

    def turn(i, carry):
        tokens_t[:, lanes(i * 256, 256)] = tokens[rows(i * 256, 256), :].T
        return carry

    lax.fori_loop(0, 4, turn, 0)
    bias_sum[...] = jnp.zeros((8, 1024), F32)

    def edge_chunk(c):
        span = pl.ds(pl.multiple_of(c * CHUNK, CHUNK), CHUNK)
        for slot in (1, 2, 3, 4):
            near_copy(c, slot).wait_recv()

        @pl.when(c < N_CHUNK - 2)
        def _():
            send_near(c + 2)

        def token_block(tb, carry):
            here = rows(tb * 512, 512)
            plain = dot(tokens[here, :], w_src[:, span]) + bias_ref[:, span]
            total = jnp.zeros((512, CHUNK), F32)
            both = dot(onehot[rows(tb * 1024, 1024), :], near[c])
            for k in range(2):
                there = rows((tb * 2 + k) * 512, 512)
                found = both[k * 512 : k * 512 + 512]
                preact = plain + found[:, :CHUNK]
                sigma = 0.5 * jnp.tanh(0.5 * preact) + 0.5
                act = preact * sigma
                grad = found[:, CHUNK:] * (sigma + act * (1.0 - sigma))
                edges[there, :CHUNK] = act.astype(BF16)
                edges[there, CHUNK:] = grad.astype(BF16)
                total = total + grad
            back[here, span] = total.astype(BF16)
            bias_sum[:, span] += jnp.sum(total.reshape(64, 8, CHUNK), axis=0)
            return carry

        lax.fori_loop(0, 2, token_block, 0, unroll=2)

        part[c] = dot(onehot_t[...], edges[...]).astype(BF16)
        for slot in (1, 2, 3, 4):
            part_copy(c, slot).start()

    def source_chunk(c):
        span = pl.ds(pl.multiple_of(c * CHUNK, CHUNK), CHUNK)
        value = dot(tokens_t[...], back[:, span])
        grads[0, :, :, :, :, span] = value.astype(BF16).reshape(4, 4, 4, 16, CHUNK)
        pair_copy(0, c).start()

    def node_chunk(c):
        span = pl.ds(pl.multiple_of(c * CHUNK, CHUNK), CHUNK)
        total = part[c, :NODE].astype(F32)
        for slot in (1, 2, 3, 4):
            part_copy(c, facing[slot]).wait_recv()
            total = total + rpart[c, slot - 1].astype(F32)
        total = total.astype(BF16)
        nsum[:, span] = total[:, :CHUNK]
        nback[:, span] = total[:, CHUNK:]

        value = dot(nodes_t[...], nback[:, span])
        grads[1, :, :, :, :, span] = value.astype(BF16).reshape(4, 4, 4, 16, CHUNK)
        pair_copy(1, c).start()
        value = dot_rows(nsum[:, span], cot[...])
        grads[2, c] = value.astype(BF16).reshape(4, 4, 16, 1024)
        pair_copy(2, c).start()

    def pair_add(m, c):
        pair_copy(m, c).wait_recv()
        if m == 2:
            acc[2, c] = grads[2, c, :, :, :, lanes(core * 512, 512)] + pair[2, c]
            return
        here = lanes(c * 128, 128)
        own = grads[m, :, :, :, :, lanes(c * CHUNK + core * 128, 128)]
        acc[m, :, :, :, :, here] = own + pair[m, :, :, :, :, here]

    def first_copy(m, c, hop):
        dim = ORDERS[m][0]
        block = (coords[dim] + hop) % 4
        if m == 2:
            source, target = acc.at[2, c, block], r1.at[2, hop - 1, c]
        else:
            here = lanes(c * 128, 128)
            source = acc.at[(m, *pick({dim: block}), slice(None), here)]
            target = r1.at[m, hop - 1, :, :, :, here]
        return remote(source, target, s1.at[m, c, hop - 1], v1.at[m, c, hop - 1], ring[dim][hop - 1])

    def second_copy(m, c, n, hop):
        done, dim = ORDERS[m][:2]
        block = (coords[dim] + hop) % 4
        if m == 2:
            here = pl.ds(c, n)
            source, target = acc.at[2, here, coords[done], block], r2.at[2, hop - 1, here]
        else:
            here = lanes(c * 128, n * 128)
            source = acc.at[(m, *pick({done: coords[done], dim: block}), slice(None), here)]
            target = r2.at[m, hop - 1, :, :, here]
        return remote(source, target, s2.at[m, c, hop - 1], v2.at[m, c, hop - 1], ring[dim][hop - 1])

    def third_copy(m, hop, other):
        dim = ORDERS[m][2]
        block = (coords[dim] + hop) % 4
        slot = 3 + hop if other else hop - 1
        device = ring_twin[dim][hop] if other else ring[dim][hop - 1]
        source = fin.at[m, block, 1 - core if other else core]
        return remote(source, r3.at[m, slot], s3.at[m, slot], v3.at[m, slot], device)

    def first_send(m, c):
        pair_add(m, c)
        for hop in HOPS:
            first_copy(m, c, hop).start()

    def second_send(m, c, n):
        dim = ORDERS[m][0]
        for each in range(c, c + n):
            for hop in HOPS:
                first_copy(m, each, hop).wait_recv()
        if m == 2:
            here = pl.ds(c, n)
            total = acc[2, here, coords[dim]].astype(F32)
            for slot in range(3):
                total = total + r1[2, slot, here].astype(F32)
            acc[2, here, coords[dim]] = total.astype(BF16)
        else:
            here = lanes(c * 128, n * 128)
            where = (m, *pick({dim: coords[dim]}), slice(None), here)
            total = acc[where].astype(F32)
            for slot in range(3):
                total = total + r1[m, slot, :, :, :, here].astype(F32)
            acc[where] = total.astype(BF16)
        for hop in HOPS:
            second_copy(m, c, n, hop).start()

    def second_add(m, c, n):
        one, two = ORDERS[m][:2]
        for hop in HOPS:
            second_copy(m, c, n, hop).wait_recv()
        if m == 2:
            here = pl.ds(c, n)
            where = (2, here, coords[one], coords[two])
            total = acc[where].astype(F32)
            for slot in range(3):
                total = total + r2[2, slot, here].astype(F32)
        else:
            here = lanes(c * 128, n * 128)
            where = (m, *pick({one: coords[one], two: coords[two]}), slice(None), here)
            total = acc[where].astype(F32)
            for slot in range(3):
                total = total + r2[m, slot, :, :, here].astype(F32)
        acc[where] = total.astype(BF16)

    def third_send(m):
        one, two = ORDERS[m][:2]
        value = acc[(m, *pick({one: coords[one], two: coords[two]}))].astype(F32)
        fin[m, :, 0] = value[:, :8]
        fin[m, :, 1] = value[:, 8:]
        for hop, other in LAST:
            third_copy(m, hop, other).start()

    def third_add(m):
        for hop, other in LAST:
            third_copy(m, hop, other).wait_recv()
        own = fin[m, coords[ORDERS[m][2]], core]
        return own + r3[m, 0] + r3[m, 1] + r3[m, 2], r3[m, 3] + r3[m, 4] + r3[m, 5] + r3[m, 6]

    def chunk(c, carry):
        @pl.when(c == N_CHUNK - 1)
        def _():
            first_send(0, 1)
            first_send(1, 0)
            first_send(2, 0)

        edge_chunk(c)

        @pl.when((c > 0) & (c < N_CHUNK - 1))
        def _():
            source_chunk(c - 1)

        @pl.when(c == N_CHUNK - 2)
        def _():
            node_chunk(0)
            first_send(0, 0)

        return carry

    lax.fori_loop(0, N_CHUNK, chunk, 0)

    def bias_send(stage):
        if stage == 3:
            return [go(remote(b_acc.at[3], b_r.at[9], b_s.at[9], b_v.at[9], twin))]
        started = []
        for hop in range(3):
            slot = 3 * stage + hop
            started.append(go(remote(
                b_acc.at[stage], b_r.at[slot], b_s.at[slot], b_v.at[slot],
                ring[BIAS_ORDER[stage]][hop],
            )))
        return started

    def bias_add(stage, copies):
        total = b_acc[stage]
        for copy in copies:
            copy.wait_recv()
        for slot in range(3 * stage, 3 * stage + len(copies)):
            total = total + b_r[slot]
        return total

    def token_grad_block(i):
        here = pl.ds(i * 256, 256)
        stage[here, :] = dot_cols(back[here, :], w_src[...]).astype(BF16)
        copy = pltpu.make_async_copy(stage.at[here], token_grad_hbm.at[here], out_sem.at[i])
        copy.start()
        return copy

    for i in range(8):
        b_acc[0, i : i + 1, :] = jnp.sum(bias_sum[:, i * 128 : i * 128 + 128], axis=0, keepdims=True)
    b_copies = bias_send(0)
    source_chunk(2)
    node_chunk(1)
    source_chunk(3)
    first_send(0, 2)
    first_send(1, 1)
    first_send(2, 1)
    node_chunk(2)
    first_send(0, 3)
    b_acc[1] = bias_add(0, b_copies)
    b_copies = bias_send(1)
    written = [token_grad_block(0)]
    first_send(1, 2)
    first_send(2, 2)
    node_chunk(3)
    first_send(1, 3)
    first_send(2, 3)
    second_send(0, 0, 4)
    second_send(1, 0, 3)
    second_send(2, 0, 3)
    b_acc[2] = bias_add(1, b_copies)
    b_copies = bias_send(2)
    written.append(token_grad_block(1))
    second_send(1, 3, 1)
    second_send(2, 3, 1)
    second_add(0, 0, 4)
    third_send(0)
    b_acc[3] = bias_add(2, b_copies)
    b_copies = bias_send(3)
    second_add(1, 0, 3)
    second_add(2, 0, 3)
    written.append(token_grad_block(2))
    second_add(1, 3, 1)
    third_send(1)
    second_add(2, 3, 1)
    third_send(2)
    written.append(token_grad_block(3))
    updated_ref[...] = (nodes[...].astype(F32) + dot(nsum[...], w_out[...])).astype(BF16)
    node_grad_ref[...] = (cot[...].astype(F32) + dot_cols(nback[...], w_dst[...])).astype(BF16)
    o_bias[...] = bias_add(3, b_copies)

    def settle(c, carry):
        for slot in (1, 2, 3, 4):
            near_copy(c, slot).wait_send()
            part_copy(c, slot).wait_send()
        for m in range(3):
            pair_copy(m, c).wait_send()
            for hop in HOPS:
                first_copy(m, c, hop).wait_send()
        return carry

    lax.fori_loop(0, N_CHUNK, settle, 0)
    for m, batches in enumerate((((0, 4),), ((0, 3), (3, 1)), ((0, 3), (3, 1)))):
        for c, n in batches:
            for hop in HOPS:
                second_copy(m, c, n, hop).wait_send()
    for m in range(3):
        own, other = third_add(m)
        if m == 2:
            outs[m][:, lanes(core * 512, 512)] = own
            outs[m][:, lanes((1 - core) * 512, 512)] = other
        else:
            for c in range(N_CHUNK):
                here = slice(c * 128, c * 128 + 128)
                outs[m][:, lanes(c * CHUNK + core * 128, 128)] = own[:, here]
                outs[m][:, lanes(c * CHUNK + (1 - core) * 128, 128)] = other[:, here]
    for copy in written:
        copy.wait()
    for copy in sends:
        copy.wait_send()

    for m in range(3):
        for hop, other in LAST:
            third_copy(m, hop, other).wait_send()


def finish_kernel(*refs):
    ins, b_ref, outs, o_ref, held, in_sems, out_sems = refs[:6], refs[6], refs[7:13], refs[13], refs[14:20], refs[20], refs[21]
    copies = []
    for i, (source, target) in enumerate(zip(ins, outs)):
        pieces = 4 if source.shape[0] == 1024 else 1
        size = source.shape[0] // pieces
        for piece in range(pieces):
            here = pl.ds(piece * size, size)
            copies.append((
                pltpu.make_async_copy(source.at[here], held[i].at[here], in_sems.at[i, piece]),
                pltpu.make_async_copy(held[i].at[here], target.at[here], out_sems.at[i, piece]),
            ))
    for fetch, _ in copies:
        fetch.start()
    index = lax.axis_index("region") * 8 + lax.axis_index("sub")
    turned = pltpu.roll(b_ref[...], (128 - index % 16 * 8) % 128, axis=1)
    own = lax.broadcasted_iota(jnp.int32, (8, 128), 0) == index // 16
    o_ref[...] = jnp.sum(jnp.where(own, turned, 0.0), axis=0, keepdims=True)[:, :8]
    for fetch, store in copies:
        fetch.wait()
        store.start()
    for _, store in copies:
        store.wait()


def finish(arrays, bias_sums):
    vmem = pl.BlockSpec(memory_space=pltpu.VMEM)
    hbm = pl.BlockSpec(memory_space=pl.ANY)
    *results, part_bias = pl.pallas_call(
        finish_kernel,
        out_shape=(
            *[jax.ShapeDtypeStruct(a.shape, a.dtype) for a in arrays],
            jax.ShapeDtypeStruct((1, 8), F32),
        ),
        in_specs=[hbm] * 6 + [vmem],
        out_specs=[hbm] * 6 + [vmem],
        scratch_shapes=[
            *[pltpu.VMEM(a.shape, a.dtype) for a in arrays],
            pltpu.SemaphoreType.DMA((6, 4)), pltpu.SemaphoreType.DMA((6, 4)),
        ],
        compiler_params=pltpu.CompilerParams(vmem_limit_bytes=60 * 1024 * 1024),
        name="finish",
    )(*arrays, bias_sums)
    return (*results, part_bias.reshape(8))


def body(tokens, nodes, dests, token_count, w_src, w_dst, bias, w_out, cotangent):
    dma = pltpu.SemaphoreType.DMA
    vmem = pl.BlockSpec(memory_space=pltpu.VMEM)
    hbm = pl.BlockSpec(memory_space=pl.ANY)
    slab = jax.ShapeDtypeStruct((8, 1024), F32)
    node_like = jax.ShapeDtypeStruct((NODE, 1024), BF16)
    whole = (1024, 1024)
    updated, token_grad, node_grad, o_src, o_dst, o_out, o_bias = pl.pallas_call(
        layer_kernel,
        out_shape=(
            node_like, jax.ShapeDtypeStruct(whole, BF16), node_like, slab, slab, slab,
            jax.ShapeDtypeStruct((8, 128), F32),
        ),
        in_specs=[hbm, hbm, vmem, vmem, hbm, hbm, vmem, hbm, hbm],
        out_specs=[vmem, hbm, vmem, vmem, vmem, vmem, vmem],
        scratch_shapes=[
            pltpu.VMEM(whole, BF16), pltpu.VMEM((NODE, 1024), BF16), pltpu.VMEM(whole, BF16),
            pltpu.VMEM(whole, BF16), pltpu.VMEM(whole, BF16), pltpu.VMEM((NODE, 1024), BF16),
            pltpu.VMEM(whole, BF16), pltpu.VMEM((1024, NODE), BF16), pltpu.VMEM((8, 1024), jnp.int32),
            pltpu.VMEM((2048, PAD), BF16), pltpu.VMEM((NEAR, 2048), BF16),
            pltpu.VMEM((N_CHUNK, PAD, 2 * CHUNK), BF16), pltpu.VMEM((2048, 2 * CHUNK), BF16),
            pltpu.VMEM(whole, BF16), pltpu.VMEM((N_CHUNK, NEAR, 2 * CHUNK), BF16),
            pltpu.VMEM((N_CHUNK, 4, NODE, 2 * CHUNK), BF16), pltpu.VMEM((NODE, 1024), BF16),
            pltpu.VMEM((NODE, 1024), BF16), pltpu.VMEM((3, 4, 4, 4, 16, 1024), BF16),
            pltpu.VMEM(whole, BF16), pltpu.VMEM((8, 1024), F32),
            pltpu.VMEM((3, 4, 4, 4, 16, 512), BF16),
            pltpu.VMEM((3, 4, 4, 4, 16, 512), BF16),
            pltpu.VMEM((3, 3, 4, 4, 16, 512), BF16),
            pltpu.VMEM((3, 3, 4, 16, 512), BF16),
            pltpu.VMEM((3, 7, 8, 512), F32),
            pltpu.VMEM((3, 4, 2, 8, 512), F32),
            pltpu.VMEM((4, 8, 128), F32),
            pltpu.VMEM((10, 8, 128), F32),
            dma((6,)), dma((4,)), dma((4, 4)), dma((4, 4)), dma((4, 4)), dma((4, 4)),
            dma((3, 4)), dma((3, 4)), dma((3, 4, 3)), dma((3, 4, 3)), dma((3, 4, 3)), dma((3, 4, 3)),
            dma((3, 7)), dma((3, 7)), dma((10,)), dma((10,)),
        ],
        compiler_params=pltpu.CompilerParams(
            collective_id=1, has_side_effects=True, vmem_limit_bytes=60 * 1024 * 1024
        ),
        name="layer",
    )(
        tokens, nodes, dests.T, token_count.reshape(1, 1), w_src, w_dst, bias.reshape(1, 1024), w_out, cotangent,
    )
    return finish((updated, token_grad, node_grad, o_src, o_dst, o_out), o_bias)


def solution(mesh):
    return jax.shard_map(
        body,
        mesh=mesh,
        in_specs=(
            P(("region", "sub"), None),
            P(("region", "sub"), None),
            P(("region", "sub"), None),
            P(("region", "sub")),
            P(),
            P(),
            P(),
            P(),
            P(("region", "sub"), None),
        ),
        out_specs=(
            P(("region", "sub"), None),
            P(("region", "sub"), None),
            P(("region", "sub"), None),
            P(("region", "sub"), None),
            P(("region", "sub"), None),
            P(("region", "sub"), None),
            P(("region", "sub")),
        ),
        check_vma=False,
    )
```

```python
import jax
import jax.numpy as jnp
from jax import lax
from jax.experimental import pallas as pl
from jax.experimental.pallas import tpu as pltpu
from jax.sharding import PartitionSpec as P

MESH = pl.DeviceIdType.MESH
F32, BF16 = jnp.float32, jnp.bfloat16
NODE = 160
NEAR = 5 * NODE
PAD = 896
CHUNK = 256
N_CHUNK = 4
DIMS = (0, 1, 2)
ORDERS = ((2, 0, 1), (0, 1, 2), (1, 2, 0))
BIAS_ORDER = (2, 1, 0)
HOPS = (2, 1, 3)
OWN, TWIN = pl.ds(0, NODE), pl.ds(NODE, NODE)
LAST = ((2, True), (2, False), (1, True), (3, True), (1, False), (3, False), (0, True))


def device_at(coords, core):
    return (coords[0] * 4 + coords[1], coords[2] * 2 + core)


def moved(coords, dim, value):
    return tuple(value if d == dim else c for d, c in enumerate(coords))


def pick(blocks):
    return tuple(blocks.get(d, slice(None)) for d in DIMS)


def dot(left, right):
    return jnp.dot(left, right, preferred_element_type=F32)


def dot_cols(left, right):
    return lax.dot_general(left, right, (((1,), (1,)), ((), ())), preferred_element_type=F32)


def dot_rows(left, right):
    return lax.dot_general(left, right, (((0,), (0,)), ((), ())), preferred_element_type=F32)


def lanes(start, size):
    return pl.ds(pl.multiple_of(start, 128), size)


def rows(start, size):
    return pl.ds(pl.multiple_of(start, 16), size)


def layer_kernel(
    tokens_hbm, nodes_hbm, dests_ref, count_ref, w_src_hbm, w_dst_hbm, bias_ref, w_out_hbm, cot_hbm,
    updated_ref, token_grad_hbm, node_grad_ref, o_src, o_dst, o_out, o_bias,
    tokens, nodes, w_src, w_dst, w_out, cot, tokens_t, nodes_t, ids, onehot, onehot_t, near, edges,
    back, part, rpart, nsum, nback, grads, stage, bias_sum,
    acc, pair, r1, r2, r3, fin, b_acc, b_r,
    twin_s, twin_v, in_sem, out_sem, near_s, near_v, part_s, part_v,
    pair_s, pair_v, s1, v1, s2, v2, s3, v3, b_s, b_v,
):
    region, sub = lax.axis_index("region"), lax.axis_index("sub")
    n_region, n_sub = 16, 8
    coords, core = (region // 4, region % 4, sub // 2), sub % 2
    twin = device_at(coords, 1 - core)
    ring = [
        [device_at(moved(coords, dim, (coords[dim] + hop) % 4), core) for hop in (1, 2, 3)]
        for dim in DIMS
    ]
    around = [
        (region, sub),
        ((region + n_region - 1) % n_region, sub),
        ((region + 1) % n_region, sub),
        (region, (sub + n_sub - 1) % n_sub),
        (region, (sub + 1) % n_sub),
    ]
    facing = (0, 2, 1, 4, 3)
    outs = (o_src, o_dst, o_out)
    ring_twin = [
        [device_at(moved(coords, dim, (coords[dim] + hop) % 4), 1 - core) for hop in range(4)]
        for dim in DIMS
    ]
    sends = []

    def remote(source, target, send, recv, device):
        return pltpu.make_async_remote_copy(
            src_ref=source, dst_ref=target, send_sem=send, recv_sem=recv,
            device_id=device, device_id_type=MESH,
        )

    def go(copy):
        copy.start()
        sends.append(copy)
        return copy

    loads = [
        pltpu.make_async_copy(source, target, in_sem.at[i])
        for i, (source, target) in enumerate((
            (nodes_hbm, nodes.at[OWN]), (cot_hbm, cot.at[OWN]), (w_dst_hbm, w_dst), (w_out_hbm, w_out),
            (w_src_hbm, w_src), (tokens_hbm, tokens),
        ))
    ]
    for load in loads[:4]:
        load.start()
    barrier = pltpu.get_barrier_semaphore()
    peers = [twin] + ring[0] + ring[1] + ring[2] + around[1:]
    peers += ring_twin[0][1:] + ring_twin[1][1:] + ring_twin[2][1:]
    for peer in peers:
        pl.semaphore_signal(barrier, inc=1, device_id=peer, device_id_type=MESH)

    def near_copy(c, slot):
        return remote(
            near.at[c, pl.ds(0, NODE)], near.at[c, pl.ds(slot * NODE, NODE)],
            near_s.at[c, slot - 1], near_v.at[c, slot - 1], around[facing[slot]],
        )

    def part_copy(c, slot):
        return remote(
            part.at[c, pl.ds(slot * NODE, NODE)], rpart.at[c, facing[slot] - 1],
            part_s.at[c, facing[slot] - 1], part_v.at[c, facing[slot] - 1], around[slot],
        )

    def twin_copy(i):
        ref = (nodes, cot)[i]
        return remote(ref.at[OWN], ref.at[TWIN], twin_s.at[i], twin_v.at[i], twin)

    def pair_copy(m, c):
        if m == 0:
            return remote(
                grads.at[:, :, :, :, lanes(c * CHUNK + (1 - core) * 128, 128)],
                pair.at[:, :, :, :, lanes(c * 128, 128)], pair_s.at[0, c], pair_v.at[0, c], twin,
            )
        ref = (nback, nsum)[m - 1]
        here = lanes(c * CHUNK + (1 - core) * 128, 128) if m == 1 else lanes(c * CHUNK, CHUNK)
        return remote(ref.at[OWN, here], ref.at[TWIN, here], pair_s.at[m, c], pair_v.at[m, c], twin)

    def project(c):
        span = pl.ds(pl.multiple_of(c * CHUNK, CHUNK), CHUNK)
        near[c, :NODE, :CHUNK] = dot(nodes[:NODE], w_dst[:, span]).astype(BF16)
        near[c, :NODE, CHUNK:] = dot_cols(cot[:NODE], w_out[span, :]).astype(BF16)
        near[c, NEAR:, :] = jnp.zeros((PAD - NEAR, 2 * CHUNK), BF16)

    def send_near(c):
        for slot in (1, 2, 3, 4):
            near_copy(c, slot).start()

    def project_later(c, carry):
        project(c)
        return carry

    for load in loads[:4]:
        load.wait()
    for load in loads[4:]:
        load.start()
    project(0)
    pl.semaphore_wait(barrier, len(peers))
    send_near(0)
    for i in range(2):
        twin_copy(i).start()

    live = lax.broadcasted_iota(jnp.int32, (2, 1024), 1) < count_ref[...]
    ids[...] = jnp.zeros((8, 1024), jnp.int32)
    ids[:2] = jnp.where(live, dests_ref[...], -1)
    ids_t = ids[...].T
    base = [(around[s][0] * n_sub + around[s][1]) * NODE for s in range(5)]

    def node_ids(shape, dim):
        place = lax.broadcasted_iota(jnp.int32, shape, dim)
        value = jnp.full(shape, -2, jnp.int32)
        for s in range(4, -1, -1):
            value = jnp.where(place < (s + 1) * NODE, place + (base[s] - s * NODE), value)
        return value

    across, down = node_ids((1, PAD), 1), node_ids((NEAR, 1), 0)
    for tb in range(4):
        for k in range(2):
            here = (tb // 2 * 2 + k) * 512 + tb % 2 * 256
            onehot[here : here + 256, :] = jnp.where(
                ids_t[tb * 256 : tb * 256 + 256, k : k + 1] == across, 1.0, 0.0
            ).astype(BF16)
            onehot_t[:, here : here + 256] = jnp.where(
                down == ids[k : k + 1, tb * 256 : tb * 256 + 256], 1.0, 0.0
            ).astype(BF16)

    lax.fori_loop(1, N_CHUNK, project_later, 0)
    send_near(1)
    for i in range(2):
        twin_copy(i).wait_recv()
    nodes_t[...] = nodes[...].T
    for load in loads[4:]:
        load.wait()

    def turn(i, carry):
        tokens_t[:, lanes(i * 256, 256)] = tokens[rows(i * 256, 256), :].T
        return carry

    lax.fori_loop(0, 4, turn, 0)
    bias_sum[...] = jnp.zeros((8, 1024), F32)

    def edge_chunk(c):
        span = pl.ds(pl.multiple_of(c * CHUNK, CHUNK), CHUNK)
        for slot in (1, 2, 3, 4):
            near_copy(c, slot).wait_recv()

        @pl.when(c < N_CHUNK - 2)
        def _():
            send_near(c + 2)

        def token_block(tb, carry):
            here = rows(tb * 512, 512)
            plain = dot(tokens[here, :], w_src[:, span]) + bias_ref[:, span]
            total = jnp.zeros((512, CHUNK), F32)
            both = dot(onehot[rows(tb * 1024, 1024), :], near[c])
            for k in range(2):
                there = rows((tb * 2 + k) * 512, 512)
                found = both[k * 512 : k * 512 + 512]
                preact = plain + found[:, :CHUNK]
                sigma = 0.5 * jnp.tanh(0.5 * preact) + 0.5
                act = preact * sigma
                grad = found[:, CHUNK:] * (sigma + act * (1.0 - sigma))
                edges[there, :CHUNK] = act.astype(BF16)
                edges[there, CHUNK:] = grad.astype(BF16)
                total = total + grad
            back[here, span] = total.astype(BF16)
            bias_sum[:, span] += jnp.sum(total.reshape(64, 8, CHUNK), axis=0)
            return carry

        lax.fori_loop(0, 2, token_block, 0, unroll=2)

        part[c] = dot(onehot_t[...], edges[...]).astype(BF16)
        for slot in (1, 2, 3, 4):
            part_copy(c, slot).start()

    def source_chunk(c):
        span = pl.ds(pl.multiple_of(c * CHUNK, CHUNK), CHUNK)
        value = dot(tokens_t[...], back[:, span])
        grads[:, :, :, :, span] = value.astype(BF16).reshape(4, 4, 4, 16, CHUNK)
        pair_copy(0, c).start()

    def node_chunk(c):
        span = pl.ds(pl.multiple_of(c * CHUNK, CHUNK), CHUNK)
        total = part[c, :NODE].astype(F32)
        for slot in (1, 2, 3, 4):
            part_copy(c, facing[slot]).wait_recv()
            total = total + rpart[c, slot - 1].astype(F32)
        total = total.astype(BF16)
        nsum[:NODE, span] = total[:, :CHUNK]
        nback[:NODE, span] = total[:, CHUNK:]
        pair_copy(1, c).start()
        pair_copy(2, c).start()

    def pair_add(m, c):
        pair_copy(m, c).wait_recv()
        here, mine = lanes(c * 128, 128), lanes(c * CHUNK + core * 128, 128)
        if m == 0:
            acc[0, :, :, :, :, here] = grads[:, :, :, :, mine] + pair[:, :, :, :, here]
        elif m == 1:
            value = dot(nodes_t[...], nback[:, mine])
            acc[1, :, :, :, :, here] = value.astype(BF16).reshape(4, 4, 4, 16, 128)
        else:
            value = dot_rows(nsum[:, lanes(c * CHUNK, CHUNK)], cot[:, lanes(core * 512, 512)])
            acc[2, c] = value.astype(BF16).reshape(4, 4, 16, 512)

    def first_copy(m, c, hop):
        dim = ORDERS[m][0]
        block = (coords[dim] + hop) % 4
        if m == 2:
            source, target = acc.at[2, c, block], r1.at[2, hop - 1, c]
        else:
            here = lanes(c * 128, 128)
            source = acc.at[(m, *pick({dim: block}), slice(None), here)]
            target = r1.at[m, hop - 1, :, :, :, here]
        return remote(source, target, s1.at[m, c, hop - 1], v1.at[m, c, hop - 1], ring[dim][hop - 1])

    def second_copy(m, c, n, hop):
        done, dim = ORDERS[m][:2]
        block = (coords[dim] + hop) % 4
        if m == 2:
            here = pl.ds(c, n)
            source, target = acc.at[2, here, coords[done], block], r2.at[2, hop - 1, here]
        else:
            here = lanes(c * 128, n * 128)
            source = acc.at[(m, *pick({done: coords[done], dim: block}), slice(None), here)]
            target = r2.at[m, hop - 1, :, :, here]
        return remote(source, target, s2.at[m, c, hop - 1], v2.at[m, c, hop - 1], ring[dim][hop - 1])

    def third_copy(m, hop, other):
        dim = ORDERS[m][2]
        block = (coords[dim] + hop) % 4
        slot = 3 + hop if other else hop - 1
        device = ring_twin[dim][hop] if other else ring[dim][hop - 1]
        source = fin.at[m, block, 1 - core if other else core]
        return remote(source, r3.at[m, slot], s3.at[m, slot], v3.at[m, slot], device)

    def first_send(m, c):
        pair_add(m, c)
        for hop in HOPS:
            first_copy(m, c, hop).start()

    def second_send(m, c, n):
        dim = ORDERS[m][0]
        for each in range(c, c + n):
            for hop in HOPS:
                first_copy(m, each, hop).wait_recv()
        if m == 2:
            here = pl.ds(c, n)
            total = acc[2, here, coords[dim]].astype(F32)
            for slot in range(3):
                total = total + r1[2, slot, here].astype(F32)
            acc[2, here, coords[dim]] = total.astype(BF16)
        else:
            here = lanes(c * 128, n * 128)
            where = (m, *pick({dim: coords[dim]}), slice(None), here)
            total = acc[where].astype(F32)
            for slot in range(3):
                total = total + r1[m, slot, :, :, :, here].astype(F32)
            acc[where] = total.astype(BF16)
        for hop in HOPS:
            second_copy(m, c, n, hop).start()

    def second_add(m, c, n):
        one, two = ORDERS[m][:2]
        for hop in HOPS:
            second_copy(m, c, n, hop).wait_recv()
        if m == 2:
            here = pl.ds(c, n)
            where = (2, here, coords[one], coords[two])
            total = acc[where].astype(F32)
            for slot in range(3):
                total = total + r2[2, slot, here].astype(F32)
        else:
            here = lanes(c * 128, n * 128)
            where = (m, *pick({one: coords[one], two: coords[two]}), slice(None), here)
            total = acc[where].astype(F32)
            for slot in range(3):
                total = total + r2[m, slot, :, :, here].astype(F32)
        acc[where] = total.astype(BF16)

    def third_send(m):
        one, two = ORDERS[m][:2]
        value = acc[(m, *pick({one: coords[one], two: coords[two]}))].astype(F32)
        fin[m, :, 0] = value[:, :8]
        fin[m, :, 1] = value[:, 8:]
        for hop, other in LAST:
            third_copy(m, hop, other).start()

    def third_add(m):
        for hop, other in LAST:
            third_copy(m, hop, other).wait_recv()
        own = fin[m, coords[ORDERS[m][2]], core]
        return own + r3[m, 0] + r3[m, 1] + r3[m, 2], r3[m, 3] + r3[m, 4] + r3[m, 5] + r3[m, 6]

    def chunk(c, carry):
        @pl.when(c == N_CHUNK - 1)
        def _():
            node_chunk(1)
            first_send(0, 1)
            first_send(1, 0)
            first_send(2, 0)

        edge_chunk(c)

        @pl.when((c > 0) & (c < N_CHUNK - 1))
        def _():
            source_chunk(c - 1)

        @pl.when(c == N_CHUNK - 2)
        def _():
            node_chunk(0)
            first_send(0, 0)

        return carry

    lax.fori_loop(0, N_CHUNK, chunk, 0)

    def bias_send(stage):
        if stage == 3:
            return [go(remote(b_acc.at[3], b_r.at[9], b_s.at[9], b_v.at[9], twin))]
        started = []
        for hop in range(3):
            slot = 3 * stage + hop
            started.append(go(remote(
                b_acc.at[stage], b_r.at[slot], b_s.at[slot], b_v.at[slot],
                ring[BIAS_ORDER[stage]][hop],
            )))
        return started

    def bias_add(stage, copies):
        total = b_acc[stage]
        for copy in copies:
            copy.wait_recv()
        for slot in range(3 * stage, 3 * stage + len(copies)):
            total = total + b_r[slot]
        return total

    def token_grad_block(i):
        here = pl.ds(i * 256, 256)
        stage[here, :] = dot_cols(back[here, :], w_src[...]).astype(BF16)
        copy = pltpu.make_async_copy(stage.at[here], token_grad_hbm.at[here], out_sem.at[i])
        copy.start()
        return copy

    for i in range(8):
        b_acc[0, i : i + 1, :] = jnp.sum(bias_sum[:, i * 128 : i * 128 + 128], axis=0, keepdims=True)
    b_copies = bias_send(0)
    first_send(1, 1)
    first_send(2, 1)
    node_chunk(2)
    source_chunk(2)
    source_chunk(3)
    first_send(1, 2)
    first_send(2, 2)
    first_send(0, 2)
    first_send(0, 3)
    b_acc[1] = bias_add(0, b_copies)
    b_copies = bias_send(1)
    written = [token_grad_block(0)]
    node_chunk(3)
    first_send(1, 3)
    first_send(2, 3)
    second_send(0, 0, 4)
    second_send(1, 0, 3)
    second_send(2, 0, 3)
    b_acc[2] = bias_add(1, b_copies)
    b_copies = bias_send(2)
    written.append(token_grad_block(1))
    second_send(1, 3, 1)
    second_send(2, 3, 1)
    second_add(0, 0, 4)
    third_send(0)
    b_acc[3] = bias_add(2, b_copies)
    b_copies = bias_send(3)
    second_add(1, 0, 3)
    second_add(2, 0, 3)
    written.append(token_grad_block(2))
    second_add(1, 3, 1)
    third_send(1)
    second_add(2, 3, 1)
    third_send(2)
    written.append(token_grad_block(3))
    updated_ref[...] = (nodes[:NODE].astype(F32) + dot(nsum[:NODE], w_out[...])).astype(BF16)
    node_grad_ref[...] = (cot[:NODE].astype(F32) + dot_cols(nback[:NODE], w_dst[...])).astype(BF16)
    o_bias[...] = bias_add(3, b_copies)

    def settle(c, carry):
        for slot in (1, 2, 3, 4):
            near_copy(c, slot).wait_send()
            part_copy(c, slot).wait_send()
        for m in range(3):
            pair_copy(m, c).wait_send()
            for hop in HOPS:
                first_copy(m, c, hop).wait_send()
        return carry

    lax.fori_loop(0, N_CHUNK, settle, 0)
    for i in range(2):
        twin_copy(i).wait_send()
    for m, batches in enumerate((((0, 4),), ((0, 3), (3, 1)), ((0, 3), (3, 1)))):
        for c, n in batches:
            for hop in HOPS:
                second_copy(m, c, n, hop).wait_send()
    for m in range(3):
        own, other = third_add(m)
        if m == 2:
            outs[m][:, lanes(core * 512, 512)] = own
            outs[m][:, lanes((1 - core) * 512, 512)] = other
        else:
            for c in range(N_CHUNK):
                here = slice(c * 128, c * 128 + 128)
                outs[m][:, lanes(c * CHUNK + core * 128, 128)] = own[:, here]
                outs[m][:, lanes(c * CHUNK + (1 - core) * 128, 128)] = other[:, here]
    for copy in written:
        copy.wait()
    for copy in sends:
        copy.wait_send()

    for m in range(3):
        for hop, other in LAST:
            third_copy(m, hop, other).wait_send()


def finish_kernel(*refs):
    ins, b_ref, outs, o_ref, held, in_sems, out_sems = refs[:6], refs[6], refs[7:13], refs[13], refs[14:20], refs[20], refs[21]
    copies = []
    for i, (source, target) in enumerate(zip(ins, outs)):
        pieces = 4 if source.shape[0] == 1024 else 1
        size = source.shape[0] // pieces
        for piece in range(pieces):
            here = pl.ds(piece * size, size)
            copies.append((
                pltpu.make_async_copy(source.at[here], held[i].at[here], in_sems.at[i, piece]),
                pltpu.make_async_copy(held[i].at[here], target.at[here], out_sems.at[i, piece]),
            ))
    for fetch, _ in copies:
        fetch.start()
    index = lax.axis_index("region") * 8 + lax.axis_index("sub")
    turned = pltpu.roll(b_ref[...], (128 - index % 16 * 8) % 128, axis=1)
    own = lax.broadcasted_iota(jnp.int32, (8, 128), 0) == index // 16
    o_ref[...] = jnp.sum(jnp.where(own, turned, 0.0), axis=0, keepdims=True)[:, :8]
    for fetch, store in copies:
        fetch.wait()
        store.start()
    for _, store in copies:
        store.wait()


def finish(arrays, bias_sums):
    vmem = pl.BlockSpec(memory_space=pltpu.VMEM)
    hbm = pl.BlockSpec(memory_space=pl.ANY)
    *results, part_bias = pl.pallas_call(
        finish_kernel,
        out_shape=(
            *[jax.ShapeDtypeStruct(a.shape, a.dtype) for a in arrays],
            jax.ShapeDtypeStruct((1, 8), F32),
        ),
        in_specs=[hbm] * 6 + [vmem],
        out_specs=[hbm] * 6 + [vmem],
        scratch_shapes=[
            *[pltpu.VMEM(a.shape, a.dtype) for a in arrays],
            pltpu.SemaphoreType.DMA((6, 4)), pltpu.SemaphoreType.DMA((6, 4)),
        ],
        compiler_params=pltpu.CompilerParams(vmem_limit_bytes=60 * 1024 * 1024),
        name="finish",
    )(*arrays, bias_sums)
    return (*results, part_bias.reshape(8))


def body(tokens, nodes, dests, token_count, w_src, w_dst, bias, w_out, cotangent):
    dma = pltpu.SemaphoreType.DMA
    vmem = pl.BlockSpec(memory_space=pltpu.VMEM)
    hbm = pl.BlockSpec(memory_space=pl.ANY)
    slab = jax.ShapeDtypeStruct((8, 1024), F32)
    node_like = jax.ShapeDtypeStruct((NODE, 1024), BF16)
    whole = (1024, 1024)
    updated, token_grad, node_grad, o_src, o_dst, o_out, o_bias = pl.pallas_call(
        layer_kernel,
        out_shape=(
            node_like, jax.ShapeDtypeStruct(whole, BF16), node_like, slab, slab, slab,
            jax.ShapeDtypeStruct((8, 128), F32),
        ),
        in_specs=[hbm, hbm, vmem, vmem, hbm, hbm, vmem, hbm, hbm],
        out_specs=[vmem, hbm, vmem, vmem, vmem, vmem, vmem],
        scratch_shapes=[
            pltpu.VMEM(whole, BF16), pltpu.VMEM((2 * NODE, 1024), BF16), pltpu.VMEM(whole, BF16),
            pltpu.VMEM(whole, BF16), pltpu.VMEM(whole, BF16), pltpu.VMEM((2 * NODE, 1024), BF16),
            pltpu.VMEM(whole, BF16), pltpu.VMEM((1024, 2 * NODE), BF16), pltpu.VMEM((8, 1024), jnp.int32),
            pltpu.VMEM((2048, PAD), BF16), pltpu.VMEM((NEAR, 2048), BF16),
            pltpu.VMEM((N_CHUNK, PAD, 2 * CHUNK), BF16), pltpu.VMEM((2048, 2 * CHUNK), BF16),
            pltpu.VMEM(whole, BF16), pltpu.VMEM((N_CHUNK, NEAR, 2 * CHUNK), BF16),
            pltpu.VMEM((N_CHUNK, 4, NODE, 2 * CHUNK), BF16), pltpu.VMEM((2 * NODE, 1024), BF16),
            pltpu.VMEM((2 * NODE, 1024), BF16), pltpu.VMEM((4, 4, 4, 16, 1024), BF16),
            pltpu.VMEM(whole, BF16), pltpu.VMEM((8, 1024), F32),
            pltpu.VMEM((3, 4, 4, 4, 16, 512), BF16),
            pltpu.VMEM((4, 4, 4, 16, 512), BF16),
            pltpu.VMEM((3, 3, 4, 4, 16, 512), BF16),
            pltpu.VMEM((3, 3, 4, 16, 512), BF16),
            pltpu.VMEM((3, 7, 8, 512), F32),
            pltpu.VMEM((3, 4, 2, 8, 512), F32),
            pltpu.VMEM((4, 8, 128), F32),
            pltpu.VMEM((10, 8, 128), F32),
            dma((2,)), dma((2,)), dma((6,)), dma((4,)), dma((4, 4)), dma((4, 4)), dma((4, 4)), dma((4, 4)),
            dma((3, 4)), dma((3, 4)), dma((3, 4, 3)), dma((3, 4, 3)), dma((3, 4, 3)), dma((3, 4, 3)),
            dma((3, 7)), dma((3, 7)), dma((10,)), dma((10,)),
        ],
        compiler_params=pltpu.CompilerParams(
            collective_id=1, has_side_effects=True, vmem_limit_bytes=60 * 1024 * 1024
        ),
        name="layer",
    )(
        tokens, nodes, dests.T, token_count.reshape(1, 1), w_src, w_dst, bias.reshape(1, 1024), w_out, cotangent,
    )
    return finish((updated, token_grad, node_grad, o_src, o_dst, o_out), o_bias)


def solution(mesh):
    return jax.shard_map(
        body,
        mesh=mesh,
        in_specs=(
            P(("region", "sub"), None),
            P(("region", "sub"), None),
            P(("region", "sub"), None),
            P(("region", "sub")),
            P(),
            P(),
            P(),
            P(),
            P(("region", "sub"), None),
        ),
        out_specs=(
            P(("region", "sub"), None),
            P(("region", "sub"), None),
            P(("region", "sub"), None),
            P(("region", "sub"), None),
            P(("region", "sub"), None),
            P(("region", "sub"), None),
            P(("region", "sub")),
        ),
        check_vma=False,
    )
```
